32 devices in a mesh: groups: 2 (over x), row: 8 (over z, y), col: 2 (over core).
Axes of the slice: x: 2, y: 2, z: 4, core: 2. Of those that a mesh axis runs over, the one named last changes fastest.
Arguments:
- pair_repr: bfloat16 [64, 32, 128], P(('groups', 'row'), 'col'), parts along dimension 0, may hold values from -6 to 6
- in_gain: float32 [128], replicated, may hold values from 0.5 to 1.5
- in_bias: float32 [128], replicated, may hold values from -0.5 to 0.5
- left_gate_w: bfloat16 [128, 128], replicated, may hold values from -0.5 to 0.5
- left_w: bfloat16 [128, 128], replicated, may hold values from -0.5 to 0.5
- right_gate_w: bfloat16 [128, 128], replicated, may hold values from -0.5 to 0.5
- right_w: bfloat16 [128, 128], replicated, may hold values from -0.5 to 0.5
- out_gate_w: bfloat16 [128, 128], replicated, may hold values from -0.5 to 0.5
- mid_gain: float32 [128], replicated, may hold values from 0.5 to 1.5
- mid_bias: float32 [128], replicated, may hold values from -0.5 to 0.5
- out_w: bfloat16 [128, 128], replicated, may hold values from -0.5 to 0.5
Outputs:
- update: bfloat16 [64, 32, 128], P(('groups', 'row'), 'col'), parts along dimension 0
The draws below stay inside these ranges and needn't reach their ends.
There are 2 independent parts, one for each index of `groups`. The reference program is written for one: setup_inputs(seed, part) draws one part's arguments, and reference() takes and returns one part's arrays. A program takes and returns all parts, laid end to end along the dimension named above; an argument that names none is the same for every part. Nothing has to cross between parts.
All inputs are finite; a program needn't handle non-finite values.
Results may differ from the reference program's by a relative error of at most 0.015.
Values may be sent and summed in bfloat16 or wider, within the bound.
No kernel may reach another device: no remote copies, remote signals or barrier semaphores. Data moves between devices by JAX's collectives and lax.ppermute only.
A program may use at most 64 MiB of HBM per device.

```python
import jax
import jax.numpy as jnp
from jax import lax

C = 128
HID = 128
TOKENS = 32


def steps_of(own_key, dims, split, smallest, largest):
    def one(position, shards_of):
        draws = jax.random.uniform(jax.random.fold_in(jax.random.fold_in(own_key, 6), position), (shards_of,), jnp.float32, smallest / len(split), largest / len(split))
        return jnp.repeat(jnp.exp(draws), dims[position] // shards_of).reshape((-1,) + (1,) * (len(dims) - position - 1))

    factor_of = one(*split[0])
    for cut in split[1:]:
        factor_of = factor_of * one(*cut)
    return factor_of


def scatter_about(rng, extent, deviation, limit, shards=(), kind=jnp.bfloat16):
    gain = steps_of(rng, extent, shards, -0.22, 0.18) if shards else 1.0
    values = jax.random.normal(rng, extent, jnp.float32) * deviation * gain
    return jnp.minimum(jnp.maximum(values, -limit), limit).astype(kind)


def setup_inputs(seed: int = 0, part: int = 0) -> dict:
    keys = jax.random.split(jax.random.key(seed), 12)
    own_keys = jax.random.split(jax.random.fold_in(keys[11], part), 12)
    pair_repr = scatter_about(own_keys[0], (TOKENS, TOKENS, C), 1.0, 6.0, ((0, 8), (1, 2)))
    in_gain = jnp.clip(1.0 + 0.1 * jax.random.normal(keys[1], (C,), jnp.float32), 0.5, 1.5)
    in_bias = jnp.clip(jax.random.uniform(keys[2], (C,), jnp.float32, -0.5, 0.5), -0.5, 0.5)
    left_gate_w = scatter_about(keys[3], (C, HID), C ** -0.5, 0.5)
    left_w = scatter_about(keys[4], (C, HID), C ** -0.5, 0.5)
    right_gate_w = scatter_about(keys[5], (C, HID), C ** -0.5, 0.5)
    right_w = scatter_about(keys[6], (C, HID), C ** -0.5, 0.5)
    out_gate_w = scatter_about(keys[7], (C, C), C ** -0.5, 0.5)
    mid_gain = jnp.clip(1.0 + 0.1 * jax.random.normal(keys[8], (HID,), jnp.float32), 0.5, 1.5)
    mid_bias = jnp.clip(jax.random.uniform(keys[9], (HID,), jnp.float32, -0.5, 0.5), -0.5, 0.5)
    out_w = scatter_about(keys[10], (HID, C), HID ** -0.5, 0.5)
    return dict(pair_repr=pair_repr, in_gain=in_gain, in_bias=in_bias, left_gate_w=left_gate_w, left_w=left_w, right_gate_w=right_gate_w, right_w=right_w, out_gate_w=out_gate_w, mid_gain=mid_gain, mid_bias=mid_bias, out_w=out_w)


def layer_norm(values, norm_gain, norm_bias):
    average = lax.optimization_barrier(jnp.mean(values, axis=-1, keepdims=True))
    centred = values - average
    variance = lax.optimization_barrier(jnp.mean(centred * centred, axis=-1, keepdims=True))
    return centred / jnp.sqrt(variance + 1e-05) * norm_gain + norm_bias

def reference(pair_repr, in_gain, in_bias, left_gate_w, left_w, right_gate_w, right_w, out_gate_w, mid_gain, mid_bias, out_w):
    normed = layer_norm(pair_repr.astype(jnp.float32), in_gain, in_bias).astype(jnp.bfloat16)
    flattened = normed.reshape(TOKENS * TOKENS, C)
    left_side = (jax.nn.sigmoid(jnp.dot(flattened, left_gate_w, preferred_element_type=jnp.float32)) * jnp.dot(flattened, left_w, preferred_element_type=jnp.float32)).astype(jnp.bfloat16)
    right_side = (jax.nn.sigmoid(jnp.dot(flattened, right_gate_w, preferred_element_type=jnp.float32)) * jnp.dot(flattened, right_w, preferred_element_type=jnp.float32)).astype(jnp.bfloat16)
    gating = jax.nn.sigmoid(jnp.dot(flattened, out_gate_w, preferred_element_type=jnp.float32))
    left_side = left_side.reshape(TOKENS, TOKENS, HID).astype(jnp.float32)
    right_side = right_side.reshape(TOKENS, TOKENS, HID).astype(jnp.float32)
    triangle = jnp.einsum('ikh,jkh->ijh', left_side, right_side)
    middle = layer_norm(triangle, mid_gain, mid_bias).astype(jnp.bfloat16).reshape(TOKENS * TOKENS, HID)
    result = gating * jnp.dot(middle, out_w, preferred_element_type=jnp.float32)
    return result.astype(jnp.bfloat16).reshape(TOKENS, TOKENS, C)
```

```python
import functools

import jax
import jax.numpy as jnp
from jax import lax
from jax.experimental import pallas as pl
from jax.experimental.pallas import tpu as pltpu
from jax.sharding import PartitionSpec as P

GROUP = 16
TOKENS_AT_ONCE = 512


def layer_norm(values, norm_gain, norm_bias):
    average = jnp.mean(values, axis=-1, keepdims=True)
    centred = values - average
    variance = jnp.mean(centred * centred, axis=-1, keepdims=True)
    return centred * lax.rsqrt(variance + 1e-05) * norm_gain + norm_bias


def gated(normed, weights):
    both = jnp.dot(normed, weights, preferred_element_type=jnp.float32)
    hidden = both.shape[1] // 2
    product = jax.nn.sigmoid(both[:, :hidden]) * both[:, hidden:]
    return product.astype(jnp.bfloat16).astype(jnp.float32)


def kernel(
    sizes,
    place_ref,
    everything,
    own,
    in_gain,
    in_bias,
    left_gate_w,
    left_w,
    right_gate_w,
    right_w,
    out_gate_w,
    mid_gain,
    mid_bias,
    out_w,
    out,
    left_held,
    right_held,
):
    rows, cols, col_parts = sizes
    depth = cols * col_parts
    channels = own.shape[2]
    here, there = place_ref[0], place_ref[1]
    gain, bias = in_gain[...], in_bias[...]

    def normed_of(tokens):
        return layer_norm(tokens.astype(jnp.float32), gain, bias).astype(jnp.bfloat16)

    def pair_row(owner, row):
        return [everything[owner * col_parts + part, row] for part in range(col_parts)]

    left_weights = jnp.concatenate([left_gate_w[...], left_w[...]], axis=1)
    for row in range(rows):
        tokens = jnp.concatenate(pair_row(here, row), axis=0)
        left_held[pl.ds(row * depth, depth)] = gated(normed_of(tokens), left_weights)

    right_weights = jnp.concatenate([right_gate_w[...], right_w[...]], axis=1)
    mid_scale, mid_shift = mid_gain[...], mid_bias[...]
    rows_at_once = max(1, min(GROUP, TOKENS_AT_ONCE // depth))

    def one_group(group):
        for first in range(0, GROUP, rows_at_once):
            tokens = []
            for j in range(first, first + rows_at_once):
                tokens += pair_row(there + group * (GROUP // rows) + j // rows, j % rows)
            right_held[pl.ds(first * depth, rows_at_once * depth)] = gated(
                normed_of(jnp.concatenate(tokens, axis=0)), right_weights
            )

        def add(k, sums):
            right = right_held[pl.ds(k, GROUP, stride=depth)]
            return [
                sums[row] + left_held[pl.ds(row * depth + k, 1)] * right for row in range(rows)
            ]

        sums = [jnp.zeros((GROUP, channels), jnp.float32)] * rows
        if depth <= 32:
            for k in range(depth):
                sums = add(k, sums)
        else:
            sums = lax.fori_loop(0, depth, add, sums, unroll=8)
        here_cols = pl.ds(group * GROUP, GROUP)
        tokens = jnp.concatenate([own[row, here_cols] for row in range(rows)], axis=0)
        gating = jax.nn.sigmoid(
            jnp.dot(normed_of(tokens), out_gate_w[...], preferred_element_type=jnp.float32)
        )
        middle = layer_norm(jnp.concatenate(sums, axis=0), mid_scale, mid_shift)
        result = gating * jnp.dot(
            middle.astype(jnp.bfloat16), out_w[...], preferred_element_type=jnp.float32
        )
        result = result.astype(jnp.bfloat16)
        for row in range(rows):
            out[row, here_cols] = result[row * GROUP : (row + 1) * GROUP]

    groups = cols // GROUP
    if groups == 1:
        one_group(0)
    else:

        @pl.loop(0, groups)
        def _(group):
            one_group(group)


def on_device(
    pair_repr,
    in_gain,
    in_bias,
    left_gate_w,
    left_w,
    right_gate_w,
    right_w,
    out_gate_w,
    mid_gain,
    mid_bias,
    out_w,
):
    rows, cols, channels = pair_repr.shape
    hidden = left_w.shape[1]
    row_parts, col_parts = lax.axis_size("row"), lax.axis_size("col")
    parts = row_parts * col_parts
    depth = cols * col_parts
    everything = lax.all_to_all(
        jnp.broadcast_to(pair_repr, (parts,) + pair_repr.shape),
        ("row", "col"),
        split_axis=0,
        concat_axis=0,
        tiled=True,
    )
    here = lax.axis_index("row")
    there = lax.axis_index("col") * (cols // rows)
    place = jnp.stack([here, there]).astype(jnp.int32)
    vmem = pl.BlockSpec(memory_space=pltpu.VMEM)
    return pl.pallas_call(
        functools.partial(kernel, (rows, cols, col_parts)),
        out_shape=jax.ShapeDtypeStruct(pair_repr.shape, jnp.bfloat16),
        in_specs=[pl.BlockSpec(memory_space=pltpu.SMEM)] + [vmem] * 12,
        out_specs=vmem,
        scratch_shapes=[
            pltpu.VMEM((rows * depth, hidden), jnp.float32),
            pltpu.VMEM((GROUP * depth, hidden), jnp.float32),
        ],
        compiler_params=pltpu.CompilerParams(vmem_limit_bytes=48 * 1024 * 1024),
    )(
        place,
        everything,
        pair_repr,
        in_gain.reshape(1, -1),
        in_bias.reshape(1, -1),
        left_gate_w,
        left_w,
        right_gate_w,
        right_w,
        out_gate_w,
        mid_gain.reshape(1, -1),
        mid_bias.reshape(1, -1),
        out_w,
    )


def solution(mesh):
    in_specs = (P(("groups", "row"), "col", None), P(), P(), P(), P(), P(), P(), P(), P(), P(), P())
    out_specs = P(("groups", "row"), "col", None)
    return jax.shard_map(
        on_device, mesh=mesh, in_specs=in_specs, out_specs=out_specs, check_vma=False
    )
```

```python
import functools

import jax
import jax.numpy as jnp
from jax import lax
from jax.experimental import pallas as pl
from jax.experimental.pallas import tpu as pltpu
from jax.sharding import PartitionSpec as P

GROUP = 16
TOKENS_AT_ONCE = 512


def layer_norm(values, norm_gain, norm_bias):
    average = jnp.mean(values, axis=-1, keepdims=True)
    centred = values - average
    variance = jnp.mean(centred * centred, axis=-1, keepdims=True)
    return centred * lax.rsqrt(variance + 1e-05) * norm_gain + norm_bias


def gated(normed, weights):
    both = jnp.dot(normed, weights, preferred_element_type=jnp.float32)
    hidden = both.shape[1] // 2
    product = jax.nn.sigmoid(both[:, :hidden]) * both[:, hidden:]
    return product.astype(jnp.bfloat16).astype(jnp.float32)


def kernel(row_parts, col_parts, *refs):
    blocks = refs[:row_parts]
    own, other = refs[row_parts : row_parts + 2]
    (
        in_gain,
        in_bias,
        left_gate_w,
        left_w,
        right_gate_w,
        right_w,
        out_gate_w,
        mid_gain,
        mid_bias,
        out_w,
        out,
        left_held,
        right_held,
    ) = refs[row_parts + 2 :]
    rows, cols, channels = own.shape
    depth = cols * col_parts
    tokens = rows * cols
    row, col = lax.axis_index("row"), lax.axis_index("col")
    gain, bias = in_gain[...], in_bias[...]

    def normed_of(pieces):
        values = jnp.concatenate([piece[...].reshape(tokens, channels) for piece in pieces], axis=0)
        return layer_norm(values.astype(jnp.float32), gain, bias).astype(jnp.bfloat16)

    left_weights = jnp.concatenate([left_gate_w[...], left_w[...]], axis=1)
    normed = normed_of([own, other])
    left = gated(normed, left_weights)
    for piece in range(2):
        part = col if piece == 0 else 1 - col
        for a in range(rows):
            start = pl.multiple_of(a * depth + part * cols, 8)
            first = piece * tokens + a * cols
            left_held[pl.ds(start, cols)] = left[first : first + cols]
    gating = jax.nn.sigmoid(
        jnp.dot(normed[:tokens], out_gate_w[...], preferred_element_type=jnp.float32)
    )

    right_weights = jnp.concatenate([right_gate_w[...], right_w[...]], axis=1)
    at_once = max(1, TOKENS_AT_ONCE // tokens)
    for begin in range(0, row_parts, at_once):
        some = range(begin, min(begin + at_once, row_parts))
        right = gated(normed_of([blocks[turn] for turn in some]), right_weights)
        for place, turn in enumerate(some):
            sender = lax.rem(row + row_parts - turn, row_parts)
            for a in range(rows):
                j = sender // col_parts * rows + a
                start = pl.multiple_of(j * depth + sender % col_parts * cols, 8)
                first = place * tokens + a * cols
                right_held[pl.ds(start, cols)] = right[first : first + cols]

    mid_scale, mid_shift = mid_gain[...], mid_bias[...]

    def one_group(group):
        def add(k, sums):
            right = right_held[pl.ds(group * GROUP * depth + k, GROUP, stride=depth)]
            return [sums[a] + left_held[pl.ds(a * depth + k, 1)] * right for a in range(rows)]

        sums = [jnp.zeros((GROUP, channels), jnp.float32)] * rows
        if depth <= 32:
            for k in range(depth):
                sums = add(k, sums)
        else:
            sums = lax.fori_loop(0, depth, add, sums, unroll=8)
        return layer_norm(jnp.concatenate(sums, axis=0), mid_scale, mid_shift)

    groups = cols // GROUP
    middle = [one_group(group).reshape(rows, GROUP, channels) for group in range(groups)]
    middle = jnp.concatenate(middle, axis=1).reshape(tokens, channels).astype(jnp.bfloat16)
    result = gating * jnp.dot(middle, out_w[...], preferred_element_type=jnp.float32)
    out[...] = result.astype(jnp.bfloat16).reshape(rows, cols, channels)


def on_device(
    pair_repr,
    in_gain,
    in_bias,
    left_gate_w,
    left_w,
    right_gate_w,
    right_w,
    out_gate_w,
    mid_gain,
    mid_bias,
    out_w,
):
    rows, cols, channels = pair_repr.shape
    hidden = left_w.shape[1]
    row_parts, col_parts = lax.axis_size("row"), lax.axis_size("col")
    depth = cols * col_parts
    owners = cols // rows

    other = lax.ppermute(
        pair_repr,
        ("row", "col"),
        [
            (r * col_parts + c, r * col_parts + (c + 1) % col_parts)
            for r in range(row_parts)
            for c in range(col_parts)
        ],
    )
    blocks = []
    for turn in range(row_parts):
        moves = []
        for r in range(row_parts):
            for c in range(col_parts):
                sender = r % owners * col_parts + c
                target = (sender + turn) % row_parts
                moves.append((r * col_parts + c, target * col_parts + r // owners))
        blocks.append(lax.ppermute(pair_repr, ("row", "col"), moves))

    vmem = pl.BlockSpec(memory_space=pltpu.VMEM)
    return pl.pallas_call(
        functools.partial(kernel, row_parts, col_parts),
        out_shape=jax.ShapeDtypeStruct(pair_repr.shape, jnp.bfloat16),
        in_specs=[vmem] * (row_parts + 12),
        out_specs=vmem,
        scratch_shapes=[
            pltpu.VMEM((rows * depth, hidden), jnp.float32),
            pltpu.VMEM((cols * depth, hidden), jnp.float32),
        ],
        compiler_params=pltpu.CompilerParams(vmem_limit_bytes=48 * 1024 * 1024),
    )(
        *blocks,
        pair_repr,
        other,
        in_gain.reshape(1, -1),
        in_bias.reshape(1, -1),
        left_gate_w,
        left_w,
        right_gate_w,
        right_w,
        out_gate_w,
        mid_gain.reshape(1, -1),
        mid_bias.reshape(1, -1),
        out_w,
    )


def solution(mesh):
    in_specs = (P(("groups", "row"), "col", None), P(), P(), P(), P(), P(), P(), P(), P(), P(), P())
    out_specs = P(("groups", "row"), "col", None)
    return jax.shard_map(
        on_device, mesh=mesh, in_specs=in_specs, out_specs=out_specs, check_vma=False
    )
```

```python
import functools

import jax
import jax.numpy as jnp
from jax import lax
from jax.experimental import pallas as pl
from jax.experimental.pallas import tpu as pltpu
from jax.sharding import PartitionSpec as P

GROUP = 16
TOKENS_AT_ONCE = 512


def layer_norm(values, norm_gain, norm_bias):
    average = jnp.mean(values, axis=-1, keepdims=True)
    centred = values - average
    variance = jnp.mean(centred * centred, axis=-1, keepdims=True)
    return centred * lax.rsqrt(variance + 1e-05) * norm_gain + norm_bias


def gated(normed, weights):
    both = jnp.dot(normed, weights, preferred_element_type=jnp.float32)
    hidden = both.shape[1] // 2
    product = jax.nn.sigmoid(both[:, :hidden]) * both[:, hidden:]
    return product.astype(jnp.bfloat16).astype(jnp.float32)


def kernel(
    sizes,
    place_ref,
    mine,
    others,
    own,
    in_gain,
    in_bias,
    left_gate_w,
    left_w,
    right_gate_w,
    right_w,
    out_gate_w,
    mid_gain,
    mid_bias,
    out_w,
    out,
    left_held,
    right_held,
):
    rows, cols, col_parts = sizes
    depth = cols * col_parts
    channels = own.shape[2]
    here, there = place_ref[0], place_ref[1]
    gain, bias = in_gain[...], in_bias[...]

    def normed_of(tokens):
        return layer_norm(tokens.astype(jnp.float32), gain, bias).astype(jnp.bfloat16)

    def pair_row(owner, row):
        return [mine[owner, row], others[owner, row]]

    left_weights = jnp.concatenate([left_gate_w[...], left_w[...]], axis=1)
    for row in range(rows):
        tokens = jnp.concatenate(pair_row(here, row), axis=0)
        left_held[pl.ds(row * depth, depth)] = gated(normed_of(tokens), left_weights)

    right_weights = jnp.concatenate([right_gate_w[...], right_w[...]], axis=1)
    mid_scale, mid_shift = mid_gain[...], mid_bias[...]
    rows_at_once = max(1, min(GROUP, TOKENS_AT_ONCE // depth))

    def one_group(group):
        for first in range(0, GROUP, rows_at_once):
            tokens = []
            for j in range(first, first + rows_at_once):
                tokens += pair_row(there + group * (GROUP // rows) + j // rows, j % rows)
            right_held[pl.ds(first * depth, rows_at_once * depth)] = gated(
                normed_of(jnp.concatenate(tokens, axis=0)), right_weights
            )

        def add(k, sums):
            right = right_held[pl.ds(k, GROUP, stride=depth)]
            return [
                sums[row] + left_held[pl.ds(row * depth + k, 1)] * right for row in range(rows)
            ]

        sums = [jnp.zeros((GROUP, channels), jnp.float32)] * rows
        if depth <= 32:
            for k in range(depth):
                sums = add(k, sums)
        else:
            sums = lax.fori_loop(0, depth, add, sums, unroll=8)
        here_cols = pl.ds(group * GROUP, GROUP)
        tokens = jnp.concatenate([own[row, here_cols] for row in range(rows)], axis=0)
        gating = jax.nn.sigmoid(
            jnp.dot(normed_of(tokens), out_gate_w[...], preferred_element_type=jnp.float32)
        )
        middle = layer_norm(jnp.concatenate(sums, axis=0), mid_scale, mid_shift)
        result = gating * jnp.dot(
            middle.astype(jnp.bfloat16), out_w[...], preferred_element_type=jnp.float32
        )
        result = result.astype(jnp.bfloat16)
        for row in range(rows):
            out[row, here_cols] = result[row * GROUP : (row + 1) * GROUP]

    groups = cols // GROUP
    if groups == 1:
        one_group(0)
    else:

        @pl.loop(0, groups)
        def _(group):
            one_group(group)


def on_device(
    pair_repr,
    in_gain,
    in_bias,
    left_gate_w,
    left_w,
    right_gate_w,
    right_w,
    out_gate_w,
    mid_gain,
    mid_bias,
    out_w,
):
    rows, cols, channels = pair_repr.shape
    hidden = left_w.shape[1]
    row_parts, col_parts = lax.axis_size("row"), lax.axis_size("col")
    depth = cols * col_parts
    mine = lax.all_to_all(
        jnp.broadcast_to(pair_repr, (row_parts,) + pair_repr.shape),
        "row",
        split_axis=0,
        concat_axis=0,
        tiled=True,
    )
    others = lax.ppermute(mine, "col", [(0, 1), (1, 0)])
    here = lax.axis_index("row")
    there = lax.axis_index("col") * (cols // rows)
    place = jnp.stack([here, there]).astype(jnp.int32)
    vmem = pl.BlockSpec(memory_space=pltpu.VMEM)
    return pl.pallas_call(
        functools.partial(kernel, (rows, cols, col_parts)),
        out_shape=jax.ShapeDtypeStruct(pair_repr.shape, jnp.bfloat16),
        in_specs=[pl.BlockSpec(memory_space=pltpu.SMEM)] + [vmem] * 13,
        out_specs=vmem,
        scratch_shapes=[
            pltpu.VMEM((rows * depth, hidden), jnp.float32),
            pltpu.VMEM((GROUP * depth, hidden), jnp.float32),
        ],
        compiler_params=pltpu.CompilerParams(vmem_limit_bytes=48 * 1024 * 1024),
    )(
        place,
        mine,
        others,
        pair_repr,
        in_gain.reshape(1, -1),
        in_bias.reshape(1, -1),
        left_gate_w,
        left_w,
        right_gate_w,
        right_w,
        out_gate_w,
        mid_gain.reshape(1, -1),
        mid_bias.reshape(1, -1),
        out_w,
    )


def solution(mesh):
    in_specs = (P(("groups", "row"), "col", None), P(), P(), P(), P(), P(), P(), P(), P(), P(), P())
    out_specs = P(("groups", "row"), "col", None)
    return jax.shard_map(
        on_device, mesh=mesh, in_specs=in_specs, out_specs=out_specs, check_vma=False
    )
```

```python
import functools

import jax
import jax.numpy as jnp
from jax import lax
from jax.experimental import pallas as pl
from jax.experimental.pallas import tpu as pltpu
from jax.sharding import PartitionSpec as P

GROUP = 16
TOKENS_AT_ONCE = 512


def layer_norm(values, norm_gain, norm_bias):
    average = jnp.mean(values, axis=-1, keepdims=True)
    centred = values - average
    variance = jnp.mean(centred * centred, axis=-1, keepdims=True)
    return centred * lax.rsqrt(variance + 1e-05) * norm_gain + norm_bias


def gated(normed, weights):
    both = jnp.dot(normed, weights, preferred_element_type=jnp.float32)
    hidden = both.shape[1] // 2
    product = jax.nn.sigmoid(both[:, :hidden]) * both[:, hidden:]
    return product.astype(jnp.bfloat16).astype(jnp.float32)


def kernel(owners, *refs):
    blocks, own = refs[:owners], refs[owners]
    params = refs[owners + 1 : owners + 11]
    out, left_held, right_held = refs[owners + 11 : owners + 14]
    held = refs[owners + 14 : owners + 24]
    sems = refs[owners + 24]
    copies = [
        pltpu.make_async_copy(source, target, sems.at[number])
        for number, (source, target) in enumerate(zip(params, held))
    ]
    for copy in copies:
        copy.start()
    (
        in_gain,
        in_bias,
        left_gate_w,
        left_w,
        right_gate_w,
        right_w,
        out_gate_w,
        mid_gain,
        mid_bias,
        out_w,
    ) = held
    col_parts, rows, cols, channels = own.shape
    depth = cols * col_parts
    tokens = rows * depth
    row, col = lax.axis_index("row"), lax.axis_index("col")
    for copy in copies:
        copy.wait()
    gain, bias = in_gain[...], in_bias[...]

    def normed_of(values):
        return layer_norm(values.astype(jnp.float32), gain, bias).astype(jnp.bfloat16)

    def by_row(block):
        return [block[part, a] for a in range(rows) for part in range(col_parts)]

    left_weights = jnp.concatenate([left_gate_w[...], left_w[...]], axis=1)
    left_held[...] = gated(normed_of(jnp.concatenate(by_row(own), axis=0)), left_weights)
    gating = jax.nn.sigmoid(
        jnp.dot(
            normed_of(own[col].reshape(rows * cols, channels)),
            out_gate_w[...],
            preferred_element_type=jnp.float32,
        )
    )

    right_weights = jnp.concatenate([right_gate_w[...], right_w[...]], axis=1)
    at_once = max(1, TOKENS_AT_ONCE // tokens)
    for begin in range(0, owners, at_once):
        some = range(begin, min(begin + at_once, owners))
        pieces = [piece for turn in some for piece in by_row(blocks[turn])]
        right = gated(normed_of(jnp.concatenate(pieces, axis=0)), right_weights)
        for place, turn in enumerate(some):
            start = pl.multiple_of(lax.bitwise_xor(lax.rem(row, owners), turn) * tokens, 8)
            right_held[pl.ds(start, tokens)] = right[place * tokens : (place + 1) * tokens]

    mid_scale, mid_shift = mid_gain[...], mid_bias[...]

    def one_group(group):
        def add(k, sums):
            right = right_held[pl.ds(group * GROUP * depth + k, GROUP, stride=depth)]
            return [sums[a] + left_held[pl.ds(a * depth + k, 1)] * right for a in range(rows)]

        sums = [jnp.zeros((GROUP, channels), jnp.float32)] * rows
        if depth <= 32:
            for k in range(depth):
                sums = add(k, sums)
        else:
            sums = lax.fori_loop(0, depth, add, sums, unroll=8)
        return layer_norm(jnp.concatenate(sums, axis=0), mid_scale, mid_shift)

    groups = cols // GROUP
    middle = [one_group(group).reshape(rows, GROUP, channels) for group in range(groups)]
    middle = jnp.concatenate(middle, axis=1).reshape(rows * cols, channels).astype(jnp.bfloat16)
    result = gating * jnp.dot(middle, out_w[...], preferred_element_type=jnp.float32)
    out[...] = result.astype(jnp.bfloat16).reshape(rows, cols, channels)


def on_device(
    pair_repr,
    in_gain,
    in_bias,
    left_gate_w,
    left_w,
    right_gate_w,
    right_w,
    out_gate_w,
    mid_gain,
    mid_bias,
    out_w,
):
    rows, cols, channels = pair_repr.shape
    hidden = left_w.shape[1]
    row_parts, col_parts = lax.axis_size("row"), lax.axis_size("col")
    depth = cols * col_parts
    owners = cols // rows

    own = lax.all_gather(pair_repr, "col")
    blocks = []
    for turn in range(owners):
        moves = []
        for r in range(row_parts):
            half, place = r // owners, r % owners
            target = place ^ turn
            moves.append((r * col_parts + half, (half * owners + target) * col_parts + half))
            moves.append(
                (r * col_parts + 1 - half, ((1 - half) * owners + target) * col_parts + half)
            )
        blocks.append(lax.ppermute(own, ("row", "col"), moves))

    vmem = pl.BlockSpec(memory_space=pltpu.VMEM)
    params = (
        in_gain.reshape(1, -1),
        in_bias.reshape(1, -1),
        left_gate_w,
        left_w,
        right_gate_w,
        right_w,
        out_gate_w,
        mid_gain.reshape(1, -1),
        mid_bias.reshape(1, -1),
        out_w,
    )
    return pl.pallas_call(
        functools.partial(kernel, owners),
        out_shape=jax.ShapeDtypeStruct(pair_repr.shape, jnp.bfloat16),
        in_specs=[vmem] * (owners + 1) + [pl.BlockSpec(memory_space=pltpu.HBM)] * len(params),
        out_specs=vmem,
        scratch_shapes=[
            pltpu.VMEM((rows * depth, hidden), jnp.float32),
            pltpu.VMEM((cols * depth, hidden), jnp.float32),
        ]
        + [pltpu.VMEM(param.shape, param.dtype) for param in params]
        + [pltpu.SemaphoreType.DMA((len(params),))],
        compiler_params=pltpu.CompilerParams(vmem_limit_bytes=48 * 1024 * 1024),
    )(*blocks, own, *params)


def solution(mesh):
    in_specs = (P(("groups", "row"), "col", None), P(), P(), P(), P(), P(), P(), P(), P(), P(), P())
    out_specs = P(("groups", "row"), "col", None)
    return jax.shard_map(
        on_device, mesh=mesh, in_specs=in_specs, out_specs=out_specs, check_vma=False
    )
```

```python
import functools

import jax
import jax.numpy as jnp
from jax import lax
from jax.experimental import pallas as pl
from jax.experimental.pallas import tpu as pltpu
from jax.sharding import PartitionSpec as P

GROUP = 16
TOKENS_AT_ONCE = 512
VMEM_LIMIT = 48 * 1024 * 1024


def layer_norm(values, norm_gain, norm_bias):
    average = jnp.mean(values, axis=-1, keepdims=True)
    centred = values - average
    variance = jnp.mean(centred * centred, axis=-1, keepdims=True)
    return centred * lax.rsqrt(variance + 1e-05) * norm_gain + norm_bias


def gated(normed, weights):
    both = jnp.dot(normed, weights, preferred_element_type=jnp.float32)
    hidden = both.shape[1] // 2
    product = jax.nn.sigmoid(both[:, :hidden]) * both[:, hidden:]
    return product.astype(jnp.bfloat16).astype(jnp.float32)


def by_row(block):
    return [block[part, a] for a in range(block.shape[1]) for part in range(block.shape[0])]


def own_rows(
    own,
    in_gain,
    in_bias,
    left_gate_w,
    left_w,
    right_gate_w,
    right_w,
    out_gate_w,
    mid_gain,
    mid_bias,
    out_w,
    left_out,
    gating_out,
    right_weights,
    last_weights,
    vectors,
):
    rows, cols, channels = own.shape[1:]
    gain, bias = in_gain[...], in_bias[...]
    for place, vector in enumerate((gain, bias, mid_gain[...], mid_bias[...])):
        vectors[place : place + 1] = vector
    right_weights[...] = jnp.concatenate([right_gate_w[...], right_w[...]], axis=1)
    last_weights[...] = out_w[...]

    def normed_of(values):
        return layer_norm(values.astype(jnp.float32), gain, bias).astype(jnp.bfloat16)

    left_weights = jnp.concatenate([left_gate_w[...], left_w[...]], axis=1)
    left_out[...] = gated(normed_of(jnp.concatenate(by_row(own), axis=0)), left_weights)
    mine = own[lax.axis_index("col")].reshape(rows * cols, channels)
    gating_out[...] = jax.nn.sigmoid(
        jnp.dot(normed_of(mine), out_gate_w[...], preferred_element_type=jnp.float32)
    )


def triangle(owners, *refs):
    blocks = refs[:owners]
    left_held, gating, right_weights, last_weights, vectors, out, right_held = refs[owners:]
    col_parts, rows, cols, channels = blocks[0].shape
    depth = cols * col_parts
    tokens = rows * depth
    place_here = lax.rem(lax.axis_index("row"), owners)
    gain, bias = vectors[0:1], vectors[1:2]
    mid_scale, mid_shift = vectors[2:3], vectors[3:4]

    at_once = max(1, TOKENS_AT_ONCE // tokens)
    for begin in range(0, owners, at_once):
        some = range(begin, min(begin + at_once, owners))
        pieces = [piece for turn in some for piece in by_row(blocks[turn])]
        values = jnp.concatenate(pieces, axis=0).astype(jnp.float32)
        right = gated(layer_norm(values, gain, bias).astype(jnp.bfloat16), right_weights[...])
        for place, turn in enumerate(some):
            start = pl.multiple_of(lax.bitwise_xor(place_here, turn) * tokens, 8)
            right_held[pl.ds(start, tokens)] = right[place * tokens : (place + 1) * tokens]

    def one_group(group):
        def add(k, sums):
            right = right_held[pl.ds(group * GROUP * depth + k, GROUP, stride=depth)]
            return [sums[a] + left_held[pl.ds(a * depth + k, 1)] * right for a in range(rows)]

        sums = [jnp.zeros((GROUP, right_held.shape[1]), jnp.float32)] * rows
        if depth <= 32:
            for k in range(depth):
                sums = add(k, sums)
        else:
            sums = lax.fori_loop(0, depth, add, sums, unroll=8)
        return layer_norm(jnp.concatenate(sums, axis=0), mid_scale, mid_shift)

    groups = cols // GROUP
    middle = [one_group(group).reshape(rows, GROUP, -1) for group in range(groups)]
    middle = jnp.concatenate(middle, axis=1).reshape(rows * cols, -1).astype(jnp.bfloat16)
    result = gating[...] * jnp.dot(middle, last_weights[...], preferred_element_type=jnp.float32)
    out[...] = result.astype(jnp.bfloat16).reshape(rows, cols, channels)


def on_device(
    pair_repr,
    in_gain,
    in_bias,
    left_gate_w,
    left_w,
    right_gate_w,
    right_w,
    out_gate_w,
    mid_gain,
    mid_bias,
    out_w,
):
    rows, cols, channels = pair_repr.shape
    hidden = left_w.shape[1]
    row_parts, col_parts = lax.axis_size("row"), lax.axis_size("col")
    depth = cols * col_parts
    owners = cols // rows

    own = lax.all_gather(pair_repr, "col")
    across, swaps = [], [[] for _ in range(owners)]
    for r in range(row_parts):
        half, place = r // owners, r % owners
        across.append((r * col_parts + half, r * col_parts + half))
        facing = (1 - half) * owners + place
        across.append((r * col_parts + 1 - half, facing * col_parts + half))
        for turn in range(1, owners):
            target = half * owners + (place ^ turn)
            for c in range(col_parts):
                swaps[turn].append((r * col_parts + c, target * col_parts + c))
    mine = lax.ppermute(own, ("row", "col"), across)

    vmem = pl.BlockSpec(memory_space=pltpu.VMEM)
    f32, bf16 = jnp.float32, jnp.bfloat16
    prepared = pl.pallas_call(
        own_rows,
        name="own_rows",
        out_shape=[
            jax.ShapeDtypeStruct((rows * depth, hidden), f32),
            jax.ShapeDtypeStruct((rows * cols, channels), f32),
            jax.ShapeDtypeStruct((channels, 2 * hidden), bf16),
            jax.ShapeDtypeStruct((hidden, channels), bf16),
            jax.ShapeDtypeStruct((8, channels), f32),
        ],
        in_specs=[vmem] * 11,
        out_specs=[vmem] * 5,
        compiler_params=pltpu.CompilerParams(vmem_limit_bytes=VMEM_LIMIT),
    )(
        own,
        in_gain.reshape(1, -1),
        in_bias.reshape(1, -1),
        left_gate_w,
        left_w,
        right_gate_w,
        right_w,
        out_gate_w,
        mid_gain.reshape(1, -1),
        mid_bias.reshape(1, -1),
        out_w,
    )
    mine, *prepared = lax.optimization_barrier((mine, *prepared))
    blocks = [mine] + [lax.ppermute(mine, ("row", "col"), swap) for swap in swaps[1:]]

    return pl.pallas_call(
        functools.partial(triangle, owners),
        name="triangle",
        out_shape=jax.ShapeDtypeStruct(pair_repr.shape, bf16),
        in_specs=[vmem] * (owners + 5),
        out_specs=vmem,
        scratch_shapes=[pltpu.VMEM((cols * depth, hidden), f32)],
        compiler_params=pltpu.CompilerParams(vmem_limit_bytes=VMEM_LIMIT),
    )(*blocks, *prepared)


def solution(mesh):
    in_specs = (P(("groups", "row"), "col", None), P(), P(), P(), P(), P(), P(), P(), P(), P(), P())
    out_specs = P(("groups", "row"), "col", None)
    return jax.shard_map(
        on_device, mesh=mesh, in_specs=in_specs, out_specs=out_specs, check_vma=False
    )
```

```python
import functools

import jax
import jax.numpy as jnp
from jax import lax
from jax.experimental import pallas as pl
from jax.experimental.pallas import tpu as pltpu
from jax.sharding import PartitionSpec as P

GROUP = 16
VMEM_LIMIT = 48 * 1024 * 1024


def layer_norm(values, norm_gain, norm_bias):
    average = jnp.mean(values, axis=-1, keepdims=True)
    centred = values - average
    variance = jnp.mean(centred * centred, axis=-1, keepdims=True)
    return centred * lax.rsqrt(variance + 1e-05) * norm_gain + norm_bias


def project(*refs):
    sources, outs, held, sems = refs[:11], refs[11:15], refs[15:26], refs[26]
    copies = [
        pltpu.make_async_copy(source, target, sems.at[number])
        for number, (source, target) in enumerate(zip(sources, held))
    ]
    for copy in copies:
        copy.start()
    sides, gating_out, last_weights, vectors = outs
    (
        pair_repr,
        in_gain,
        in_bias,
        left_gate_w,
        left_w,
        right_gate_w,
        right_w,
        out_gate_w,
        mid_gain,
        mid_bias,
        out_w,
    ) = held
    rows, cols, channels = pair_repr.shape
    for copy in copies:
        copy.wait()
    values = pair_repr[...].reshape(rows * cols, channels).astype(jnp.float32)
    normed = layer_norm(values, in_gain[...], in_bias[...]).astype(jnp.bfloat16)

    def times(weights):
        return jnp.dot(normed, weights[...], preferred_element_type=jnp.float32)

    right = jax.nn.sigmoid(times(right_gate_w)) * times(right_w)
    left = jax.nn.sigmoid(times(left_gate_w)) * times(left_w)
    sides[0] = left.astype(jnp.bfloat16).reshape(sides.shape[1:])
    sides[1] = right.astype(jnp.bfloat16).reshape(sides.shape[1:])
    gating_out[...] = jax.nn.sigmoid(times(out_gate_w))
    last_weights[...] = out_w[...]
    vectors[0:1] = mid_gain[...]
    vectors[1:2] = mid_bias[...]


def join(sides, others, joined):
    col = lax.axis_index("col")
    joined[col] = sides[1]
    joined[1 - col] = others[1]


def triangle(owners, *refs):
    blocks = refs[:owners]
    sides, others, gating, last_weights, vectors, out, left_held, right_held = refs[owners:]
    col_parts, rows, cols, hidden = blocks[0].shape
    depth = cols * col_parts
    tokens = rows * depth
    place_here = lax.rem(lax.axis_index("row"), owners)
    col = lax.axis_index("col")

    for a in range(rows):
        start = pl.multiple_of(a * depth + col * cols, 8)
        left_held[pl.ds(start, cols)] = sides[0, a].astype(jnp.float32)
        start = pl.multiple_of(a * depth + (1 - col) * cols, 8)
        left_held[pl.ds(start, cols)] = others[0, a].astype(jnp.float32)
    for turn in range(owners):
        start = lax.bitwise_xor(place_here, turn) * tokens
        for a in range(rows):
            for part in range(col_parts):
                at = pl.multiple_of(start + a * depth + part * cols, 8)
                right_held[pl.ds(at, cols)] = blocks[turn][part, a].astype(jnp.float32)

    def one_group(group):
        def add(k, sums):
            right = right_held[pl.ds(group * GROUP * depth + k, GROUP, stride=depth)]
            return [sums[a] + left_held[pl.ds(a * depth + k, 1)] * right for a in range(rows)]

        sums = [jnp.zeros((GROUP, hidden), jnp.float32)] * rows
        if depth <= 32:
            for k in range(depth):
                sums = add(k, sums)
        else:
            sums = lax.fori_loop(0, depth, add, sums, unroll=8)
        return layer_norm(jnp.concatenate(sums, axis=0), vectors[0:1], vectors[1:2])

    groups = cols // GROUP
    middle = [one_group(group).reshape(rows, GROUP, hidden) for group in range(groups)]
    middle = jnp.concatenate(middle, axis=1).reshape(rows * cols, hidden).astype(jnp.bfloat16)
    result = gating[...] * jnp.dot(middle, last_weights[...], preferred_element_type=jnp.float32)
    out[...] = result.astype(jnp.bfloat16).reshape(out.shape)


def on_device(pair_repr, *params):
    rows, cols, channels = pair_repr.shape
    hidden = params[3].shape[1]
    row_parts, col_parts = lax.axis_size("row"), lax.axis_size("col")
    depth = cols * col_parts
    owners = cols // rows
    f32, bf16 = jnp.float32, jnp.bfloat16
    vmem = pl.BlockSpec(memory_space=pltpu.VMEM)
    compiler_params = pltpu.CompilerParams(vmem_limit_bytes=VMEM_LIMIT)

    sources = [pair_repr] + [p.reshape(1, -1) if p.ndim == 1 else p for p in params]
    sources = [pltpu.with_memory_space_constraint(source, pltpu.HBM) for source in sources]
    sides, gating, last_weights, vectors = pl.pallas_call(
        project,
        name="project",
        out_shape=[
            jax.ShapeDtypeStruct((2, rows, cols, hidden), bf16),
            jax.ShapeDtypeStruct((rows * cols, channels), f32),
            jax.ShapeDtypeStruct((hidden, channels), bf16),
            jax.ShapeDtypeStruct((8, hidden), f32),
        ],
        in_specs=[pl.BlockSpec(memory_space=pltpu.HBM)] * len(sources),
        out_specs=[vmem] * 4,
        scratch_shapes=[pltpu.VMEM(source.shape, source.dtype) for source in sources]
        + [pltpu.SemaphoreType.DMA((len(sources),))],
        compiler_params=compiler_params,
    )(*sources)

    others = lax.ppermute(sides, "col", [(0, 1), (1, 0)])
    joined = pl.pallas_call(
        join,
        name="join",
        out_shape=jax.ShapeDtypeStruct((col_parts, rows, cols, hidden), bf16),
        in_specs=[vmem] * 2,
        out_specs=vmem,
        compiler_params=compiler_params,
    )(sides, others)
    across, swaps = [], [[] for _ in range(owners)]
    for r in range(row_parts):
        half, place = r // owners, r % owners
        across.append((r * col_parts + half, r * col_parts + half))
        facing = (1 - half) * owners + place
        across.append((r * col_parts + 1 - half, facing * col_parts + half))
        for turn in range(1, owners):
            target = half * owners + (place ^ turn)
            for c in range(col_parts):
                swaps[turn].append((r * col_parts + c, target * col_parts + c))
    mine = lax.ppermute(joined, ("row", "col"), across)
    blocks = [mine] + [lax.ppermute(mine, ("row", "col"), swap) for swap in swaps[1:]]

    return pl.pallas_call(
        functools.partial(triangle, owners),
        name="triangle",
        out_shape=jax.ShapeDtypeStruct(pair_repr.shape, bf16),
        in_specs=[vmem] * (owners + 5),
        out_specs=vmem,
        scratch_shapes=[pltpu.VMEM((rows * depth, hidden), f32)]
        + [pltpu.VMEM((cols * depth, hidden), f32)],
        compiler_params=compiler_params,
    )(*blocks, sides, others, gating, last_weights, vectors)


def solution(mesh):
    in_specs = (P(("groups", "row"), "col", None), P(), P(), P(), P(), P(), P(), P(), P(), P(), P())
    out_specs = P(("groups", "row"), "col", None)
    return jax.shard_map(
        on_device, mesh=mesh, in_specs=in_specs, out_specs=out_specs, check_vma=False
    )
```

```python
import functools

import jax
import jax.numpy as jnp
from jax import lax
from jax.experimental import pallas as pl
from jax.experimental.pallas import tpu as pltpu
from jax.sharding import PartitionSpec as P

GROUP = 16
VMEM_LIMIT = 48 * 1024 * 1024


def layer_norm(values, norm_gain, norm_bias):
    average = jnp.mean(values, axis=-1, keepdims=True)
    centred = values - average
    variance = jnp.mean(centred * centred, axis=-1, keepdims=True)
    return centred * lax.rsqrt(variance + 1e-05) * norm_gain + norm_bias


def project(*refs):
    sources, outs, held, sems = refs[:11], refs[11:15], refs[15:26], refs[26]
    copies = [
        pltpu.make_async_copy(source, target, sems.at[number])
        for number, (source, target) in enumerate(zip(sources, held))
    ]
    for copy in copies:
        copy.start()
    sides, gating_out, last_weights, vectors = outs
    (
        pair_repr,
        in_gain,
        in_bias,
        left_gate_w,
        left_w,
        right_gate_w,
        right_w,
        out_gate_w,
        mid_gain,
        mid_bias,
        out_w,
    ) = held
    rows, cols, channels = pair_repr.shape
    for copy in copies:
        copy.wait()
    values = pair_repr[...].reshape(rows * cols, channels).astype(jnp.float32)
    normed = layer_norm(values, in_gain[...], in_bias[...]).astype(jnp.bfloat16)

    def times(weights):
        return jnp.dot(normed, weights[...], preferred_element_type=jnp.float32)

    right = jax.nn.sigmoid(times(right_gate_w)) * times(right_w)
    left = jax.nn.sigmoid(times(left_gate_w)) * times(left_w)
    sides[0] = left.astype(jnp.bfloat16).reshape(sides.shape[1:])
    sides[1] = right.astype(jnp.bfloat16).reshape(sides.shape[1:])
    gating_out[...] = jax.nn.sigmoid(times(out_gate_w))
    last_weights[...] = out_w[...]
    vectors[0:1] = mid_gain[...]
    vectors[1:2] = mid_bias[...]


def join(sides, others, joined):
    col = lax.axis_index("col")
    joined[col] = sides[1]
    joined[1 - col] = others[1]


def choose(owners, joined, crossed, mine):
    at_home = lax.axis_index("row") // owners == lax.axis_index("col")

    @pl.when(at_home)
    def _():
        mine[...] = joined[...]

    @pl.when(jnp.logical_not(at_home))
    def _():
        mine[...] = crossed[...]


def triangle(owners, *refs):
    blocks = refs[:owners]
    sides, others, gating, last_weights, vectors, out, left_held, right_held = refs[owners:]
    col_parts, rows, cols, hidden = blocks[0].shape
    depth = cols * col_parts
    tokens = rows * depth
    place_here = lax.rem(lax.axis_index("row"), owners)
    col = lax.axis_index("col")

    for a in range(rows):
        start = pl.multiple_of(a * depth + col * cols, 8)
        left_held[pl.ds(start, cols)] = sides[0, a].astype(jnp.float32)
        start = pl.multiple_of(a * depth + (1 - col) * cols, 8)
        left_held[pl.ds(start, cols)] = others[0, a].astype(jnp.float32)
    for turn in range(owners):
        start = lax.bitwise_xor(place_here, turn) * tokens
        for a in range(rows):
            for part in range(col_parts):
                at = pl.multiple_of(start + a * depth + part * cols, 8)
                right_held[pl.ds(at, cols)] = blocks[turn][part, a].astype(jnp.float32)

    def one_group(group):
        def add(k, sums):
            right = right_held[pl.ds(group * GROUP * depth + k, GROUP, stride=depth)]
            return [sums[a] + left_held[pl.ds(a * depth + k, 1)] * right for a in range(rows)]

        sums = [jnp.zeros((GROUP, hidden), jnp.float32)] * rows
        if depth <= 32:
            for k in range(depth):
                sums = add(k, sums)
        else:
            sums = lax.fori_loop(0, depth, add, sums, unroll=8)
        return layer_norm(jnp.concatenate(sums, axis=0), vectors[0:1], vectors[1:2])

    groups = cols // GROUP
    middle = [one_group(group).reshape(rows, GROUP, hidden) for group in range(groups)]
    middle = jnp.concatenate(middle, axis=1).reshape(rows * cols, hidden).astype(jnp.bfloat16)
    result = gating[...] * jnp.dot(middle, last_weights[...], preferred_element_type=jnp.float32)
    out[...] = result.astype(jnp.bfloat16).reshape(out.shape)


def on_device(pair_repr, *params):
    rows, cols, channels = pair_repr.shape
    hidden = params[3].shape[1]
    row_parts, col_parts = lax.axis_size("row"), lax.axis_size("col")
    depth = cols * col_parts
    owners = cols // rows
    f32, bf16 = jnp.float32, jnp.bfloat16
    vmem = pl.BlockSpec(memory_space=pltpu.VMEM)
    compiler_params = pltpu.CompilerParams(vmem_limit_bytes=VMEM_LIMIT)

    sources = [pair_repr] + [p.reshape(1, -1) if p.ndim == 1 else p for p in params]
    sources = [pltpu.with_memory_space_constraint(source, pltpu.HBM) for source in sources]
    sides, gating, last_weights, vectors = pl.pallas_call(
        project,
        name="project",
        out_shape=[
            jax.ShapeDtypeStruct((2, rows, cols, hidden), bf16),
            jax.ShapeDtypeStruct((rows * cols, channels), f32),
            jax.ShapeDtypeStruct((hidden, channels), bf16),
            jax.ShapeDtypeStruct((8, hidden), f32),
        ],
        in_specs=[pl.BlockSpec(memory_space=pltpu.HBM)] * len(sources),
        out_specs=[vmem] * 4,
        scratch_shapes=[pltpu.VMEM(source.shape, source.dtype) for source in sources]
        + [pltpu.SemaphoreType.DMA((len(sources),))],
        compiler_params=compiler_params,
    )(*sources)

    others = lax.ppermute(sides, "col", [(0, 1), (1, 0)])
    joined = pl.pallas_call(
        join,
        name="join",
        out_shape=jax.ShapeDtypeStruct((col_parts, rows, cols, hidden), bf16),
        in_specs=[vmem] * 2,
        out_specs=vmem,
        compiler_params=compiler_params,
    )(sides, others)
    across, swaps = [], [[] for _ in range(owners)]
    for r in range(row_parts):
        half, place = r // owners, r % owners
        facing = (1 - half) * owners + place
        across.append((r * col_parts + half, facing * col_parts + half))
        for turn in range(1, owners):
            target = half * owners + (place ^ turn)
            for c in range(col_parts):
                swaps[turn].append((r * col_parts + c, target * col_parts + c))
    crossed = lax.ppermute(joined, ("row", "col"), across)
    mine = pl.pallas_call(
        functools.partial(choose, owners),
        name="choose",
        out_shape=jax.ShapeDtypeStruct(joined.shape, bf16),
        in_specs=[vmem] * 2,
        out_specs=vmem,
        compiler_params=compiler_params,
    )(joined, crossed)
    blocks = [mine] + [lax.ppermute(mine, ("row", "col"), swap) for swap in swaps[1:]]

    return pl.pallas_call(
        functools.partial(triangle, owners),
        name="triangle",
        out_shape=jax.ShapeDtypeStruct(pair_repr.shape, bf16),
        in_specs=[vmem] * (owners + 5),
        out_specs=vmem,
        scratch_shapes=[pltpu.VMEM((rows * depth, hidden), f32)]
        + [pltpu.VMEM((cols * depth, hidden), f32)],
        compiler_params=compiler_params,
    )(*blocks, sides, others, gating, last_weights, vectors)


def solution(mesh):
    in_specs = (P(("groups", "row"), "col", None), P(), P(), P(), P(), P(), P(), P(), P(), P(), P())
    out_specs = P(("groups", "row"), "col", None)
    return jax.shard_map(
        on_device, mesh=mesh, in_specs=in_specs, out_specs=out_specs, check_vma=False
    )
```

```python
import functools

import jax
import jax.numpy as jnp
from jax import lax
from jax.experimental import pallas as pl
from jax.experimental.pallas import tpu as pltpu
from jax.sharding import PartitionSpec as P

GROUP = 16
VMEM_LIMIT = 48 * 1024 * 1024


def layer_norm(values, norm_gain, norm_bias):
    average = jnp.mean(values, axis=-1, keepdims=True)
    centred = values - average
    variance = jnp.mean(centred * centred, axis=-1, keepdims=True)
    return centred * lax.rsqrt(variance + 1e-05) * norm_gain + norm_bias


def project(*refs):
    sources, outs, held, sems = refs[:11], refs[11:15], refs[15:26], refs[26]
    copies = [
        pltpu.make_async_copy(source, target, sems.at[number])
        for number, (source, target) in enumerate(zip(sources, held))
    ]
    for copy in copies:
        copy.start()
    sides, gating_out, last_weights, vectors = outs
    (
        pair_repr,
        in_gain,
        in_bias,
        left_gate_w,
        left_w,
        right_gate_w,
        right_w,
        out_gate_w,
        mid_gain,
        mid_bias,
        out_w,
    ) = held
    rows, cols, channels = pair_repr.shape
    for copy in copies:
        copy.wait()
    values = pair_repr[...].reshape(rows * cols, channels).astype(jnp.float32)
    normed = layer_norm(values, in_gain[...], in_bias[...]).astype(jnp.bfloat16)

    def times(weights):
        return jnp.dot(normed, weights[...], preferred_element_type=jnp.float32)

    right = jax.nn.sigmoid(times(right_gate_w)) * times(right_w)
    left = jax.nn.sigmoid(times(left_gate_w)) * times(left_w)
    sides[0] = left.astype(jnp.bfloat16).reshape(sides.shape[1:])
    sides[1] = right.astype(jnp.bfloat16).reshape(sides.shape[1:])
    gating_out[...] = jax.nn.sigmoid(times(out_gate_w))
    last_weights[...] = out_w[...]
    vectors[0:1] = mid_gain[...]
    vectors[1:2] = mid_bias[...]


def join(sides, others, joined):
    col = lax.axis_index("col")
    joined[col] = sides[1]
    joined[1 - col] = others[1]


def triangle(owners, *refs):
    blocks = refs[:owners]
    sides, others, gating, last_weights, vectors, out, left_held, right_held = refs[owners:]
    col_parts, rows, cols, hidden = blocks[0].shape
    depth = cols * col_parts
    tokens = rows * depth
    row, col = lax.axis_index("row"), lax.axis_index("col")
    place_here = lax.rem(row, owners)
    place_here = jnp.where(row // owners == col, place_here, place_here ^ (owners // 2))

    for a in range(rows):
        start = pl.multiple_of(a * depth + col * cols, 8)
        left_held[pl.ds(start, cols)] = sides[0, a].astype(jnp.float32)
        start = pl.multiple_of(a * depth + (1 - col) * cols, 8)
        left_held[pl.ds(start, cols)] = others[0, a].astype(jnp.float32)
    for turn in range(owners):
        start = lax.bitwise_xor(place_here, turn) * tokens
        for a in range(rows):
            for part in range(col_parts):
                at = pl.multiple_of(start + a * depth + part * cols, 8)
                right_held[pl.ds(at, cols)] = blocks[turn][part, a].astype(jnp.float32)

    def one_group(group):
        def add(k, sums):
            right = right_held[pl.ds(group * GROUP * depth + k, GROUP, stride=depth)]
            return [sums[a] + left_held[pl.ds(a * depth + k, 1)] * right for a in range(rows)]

        sums = [jnp.zeros((GROUP, hidden), jnp.float32)] * rows
        if depth <= 32:
            for k in range(depth):
                sums = add(k, sums)
        else:
            sums = lax.fori_loop(0, depth, add, sums, unroll=8)
        return layer_norm(jnp.concatenate(sums, axis=0), vectors[0:1], vectors[1:2])

    groups = cols // GROUP
    middle = [one_group(group).reshape(rows, GROUP, hidden) for group in range(groups)]
    middle = jnp.concatenate(middle, axis=1).reshape(rows * cols, hidden).astype(jnp.bfloat16)
    result = gating[...] * jnp.dot(middle, last_weights[...], preferred_element_type=jnp.float32)
    out[...] = result.astype(jnp.bfloat16).reshape(out.shape)


def on_device(pair_repr, *params):
    rows, cols, channels = pair_repr.shape
    hidden = params[3].shape[1]
    row_parts, col_parts = lax.axis_size("row"), lax.axis_size("col")
    depth = cols * col_parts
    owners = cols // rows
    f32, bf16 = jnp.float32, jnp.bfloat16
    vmem = pl.BlockSpec(memory_space=pltpu.VMEM)
    compiler_params = pltpu.CompilerParams(vmem_limit_bytes=VMEM_LIMIT)

    sources = [pair_repr] + [p.reshape(1, -1) if p.ndim == 1 else p for p in params]
    sources = [pltpu.with_memory_space_constraint(source, pltpu.HBM) for source in sources]
    sides, gating, last_weights, vectors = pl.pallas_call(
        project,
        name="project",
        out_shape=[
            jax.ShapeDtypeStruct((2, rows, cols, hidden), bf16),
            jax.ShapeDtypeStruct((rows * cols, channels), f32),
            jax.ShapeDtypeStruct((hidden, channels), bf16),
            jax.ShapeDtypeStruct((8, hidden), f32),
        ],
        in_specs=[pl.BlockSpec(memory_space=pltpu.HBM)] * len(sources),
        out_specs=[vmem] * 4,
        scratch_shapes=[pltpu.VMEM(source.shape, source.dtype) for source in sources]
        + [pltpu.SemaphoreType.DMA((len(sources),))],
        compiler_params=compiler_params,
    )(*sources)

    others = lax.ppermute(sides, "col", [(0, 1), (1, 0)])
    joined = pl.pallas_call(
        join,
        name="join",
        out_shape=jax.ShapeDtypeStruct((col_parts, rows, cols, hidden), bf16),
        in_specs=[vmem] * 2,
        out_specs=vmem,
        compiler_params=compiler_params,
    )(sides, others)
    across, swaps = [], [[] for _ in range(owners)]
    for r in range(row_parts):
        half, place = r // owners, r % owners
        across.append((r * col_parts + half, r * col_parts + half))
        facing = (1 - half) * owners + (place ^ owners // 2)
        across.append((r * col_parts + 1 - half, facing * col_parts + half))
        for turn in range(1, owners):
            target = half * owners + (place ^ turn)
            for c in range(col_parts):
                swaps[turn].append((r * col_parts + c, target * col_parts + c))
    mine = lax.ppermute(joined, ("row", "col"), across)
    blocks = [mine] + [lax.ppermute(mine, ("row", "col"), swap) for swap in swaps[1:]]

    return pl.pallas_call(
        functools.partial(triangle, owners),
        name="triangle",
        out_shape=jax.ShapeDtypeStruct(pair_repr.shape, bf16),
        in_specs=[vmem] * (owners + 5),
        out_specs=vmem,
        scratch_shapes=[pltpu.VMEM((rows * depth, hidden), f32)]
        + [pltpu.VMEM((cols * depth, hidden), f32)],
        compiler_params=compiler_params,
    )(*blocks, sides, others, gating, last_weights, vectors)


def solution(mesh):
    in_specs = (P(("groups", "row"), "col", None), P(), P(), P(), P(), P(), P(), P(), P(), P(), P())
    out_specs = P(("groups", "row"), "col", None)
    return jax.shard_map(
        on_device, mesh=mesh, in_specs=in_specs, out_specs=out_specs, check_vma=False
    )
```

```python
import functools

import jax
import jax.numpy as jnp
from jax import lax
from jax.experimental import pallas as pl
from jax.experimental.pallas import tpu as pltpu
from jax.sharding import PartitionSpec as P

GROUP = 16
VMEM_LIMIT = 48 * 1024 * 1024


def layer_norm(values, norm_gain, norm_bias):
    average = jnp.mean(values, axis=-1, keepdims=True)
    centred = values - average
    variance = jnp.mean(centred * centred, axis=-1, keepdims=True)
    return centred * lax.rsqrt(variance + 1e-05) * norm_gain + norm_bias


def normed_of(block, gain, bias):
    values = block[...].reshape(-1, block.shape[-1]).astype(jnp.float32)
    return layer_norm(values, gain, bias).astype(jnp.bfloat16)


def gated(normed, gate_w, w):
    gate = jnp.dot(normed, gate_w, preferred_element_type=jnp.float32)
    value = jnp.dot(normed, w, preferred_element_type=jnp.float32)
    return (jax.nn.sigmoid(gate) * value).astype(jnp.bfloat16)


def project(*refs):
    sources, outs, held, sems = refs[:11], refs[11:18], refs[18:29], refs[29]
    copies = [
        pltpu.make_async_copy(source, target, sems.at[number])
        for number, (source, target) in enumerate(zip(sources, held))
    ]
    for copy in copies:
        copy.start()
    left, right, gating, right_gate_out, right_out, last_weights, vectors = outs
    (
        pair_repr,
        in_gain,
        in_bias,
        left_gate_w,
        left_w,
        right_gate_w,
        right_w,
        out_gate_w,
        mid_gain,
        mid_bias,
        out_w,
    ) = held
    for copy in copies:
        copy.wait()
    normed = normed_of(pair_repr, in_gain[...], in_bias[...])
    left[...] = gated(normed, left_gate_w[...], left_w[...]).reshape(left.shape)
    right[...] = gated(normed, right_gate_w[...], right_w[...]).reshape(right.shape)
    gate = jnp.dot(normed, out_gate_w[...], preferred_element_type=jnp.float32)
    gating[...] = jax.nn.sigmoid(gate)
    right_gate_out[...] = right_gate_w[...]
    right_out[...] = right_w[...]
    last_weights[...] = out_w[...]
    for place, vector in enumerate((in_gain, in_bias, mid_gain, mid_bias)):
        vectors[place : place + 1] = vector[...]


def lay_out(owners, crossed, right, right_gate_w, right_w, vectors, slots):
    half = lax.axis_index("row") // owners
    normed = normed_of(crossed, vectors[0:1], vectors[1:2])
    other = gated(normed, right_gate_w[...], right_w[...]).reshape(right.shape)
    mine = right[...]
    for place in range(owners):
        slots[2 * place + half] = mine
        slots[2 * place + 1 - half] = other


def triangle(
    everything, left, left_other, gating, last_weights, vectors, out, left_held, right_held
):
    rows, cols, hidden = left.shape
    parts = everything.shape[0]
    depth = 2 * cols
    col = lax.axis_index("col")

    for a in range(rows):
        start = pl.multiple_of(a * depth + col * cols, 8)
        left_held[pl.ds(start, cols)] = left[a].astype(jnp.float32)
        start = pl.multiple_of(a * depth + (1 - col) * cols, 8)
        left_held[pl.ds(start, cols)] = left_other[a].astype(jnp.float32)
    for part in range(parts):
        for a in range(rows):
            start = (part // 2 * rows + a) * depth + part % 2 * cols
            right_held[start : start + cols] = everything[part, a].astype(jnp.float32)

    def one_group(group):
        def add(k, sums):
            right = right_held[pl.ds(group * GROUP * depth + k, GROUP, stride=depth)]
            return [sums[a] + left_held[pl.ds(a * depth + k, 1)] * right for a in range(rows)]

        sums = [jnp.zeros((GROUP, hidden), jnp.float32)] * rows
        if depth <= 32:
            for k in range(depth):
                sums = add(k, sums)
        else:
            sums = lax.fori_loop(0, depth, add, sums, unroll=8)
        return layer_norm(jnp.concatenate(sums, axis=0), vectors[2:3], vectors[3:4])

    groups = cols // GROUP
    middle = [one_group(group).reshape(rows, GROUP, hidden) for group in range(groups)]
    middle = jnp.concatenate(middle, axis=1).reshape(rows * cols, hidden).astype(jnp.bfloat16)
    result = gating[...] * jnp.dot(middle, last_weights[...], preferred_element_type=jnp.float32)
    out[...] = result.astype(jnp.bfloat16).reshape(out.shape)


def on_device(pair_repr, *params):
    rows, cols, channels = pair_repr.shape
    hidden = params[3].shape[1]
    row_parts, col_parts = lax.axis_size("row"), lax.axis_size("col")
    depth = cols * col_parts
    owners = cols // rows
    f32, bf16 = jnp.float32, jnp.bfloat16
    vmem = pl.BlockSpec(memory_space=pltpu.VMEM)
    compiler_params = pltpu.CompilerParams(vmem_limit_bytes=VMEM_LIMIT)
    shape = jax.ShapeDtypeStruct

    crossed = lax.ppermute(
        pair_repr,
        ("row", "col"),
        [
            (r * col_parts + c, (r + owners) % row_parts * col_parts + c)
            for r in range(row_parts)
            for c in range(col_parts)
        ],
    )

    sources = [pair_repr] + [p.reshape(1, -1) if p.ndim == 1 else p for p in params]
    sources = [pltpu.with_memory_space_constraint(source, pltpu.HBM) for source in sources]
    left, right, gating, right_gate_w, right_w, last_weights, vectors = pl.pallas_call(
        project,
        name="project",
        out_shape=[
            shape((rows, cols, hidden), bf16),
            shape((rows, cols, hidden), bf16),
            shape((rows * cols, channels), f32),
            shape((channels, hidden), bf16),
            shape((channels, hidden), bf16),
            shape((hidden, channels), bf16),
            shape((8, hidden), f32),
        ],
        in_specs=[pl.BlockSpec(memory_space=pltpu.HBM)] * len(sources),
        out_specs=[vmem] * 7,
        scratch_shapes=[pltpu.VMEM(source.shape, source.dtype) for source in sources]
        + [pltpu.SemaphoreType.DMA((len(sources),))],
        compiler_params=compiler_params,
    )(*sources)
    left_other = lax.ppermute(left, "col", [(0, 1), (1, 0)])

    slots = pl.pallas_call(
        functools.partial(lay_out, owners),
        name="lay_out",
        out_shape=shape((2 * owners, rows, cols, hidden), bf16),
        in_specs=[vmem] * 5,
        out_specs=vmem,
        compiler_params=compiler_params,
    )(crossed, right, right_gate_w, right_w, vectors)
    members = owners * col_parts
    everything = lax.all_to_all(
        slots,
        ("row", "col"),
        split_axis=0,
        concat_axis=0,
        tiled=True,
        axis_index_groups=[
            list(range(first, first + members)) for first in range(0, 2 * members, members)
        ],
    )

    return pl.pallas_call(
        triangle,
        name="triangle",
        out_shape=shape(pair_repr.shape, bf16),
        in_specs=[vmem] * 6,
        out_specs=vmem,
        scratch_shapes=[
            pltpu.VMEM((rows * depth, hidden), f32),
            pltpu.VMEM((cols * depth, hidden), f32),
        ],
        compiler_params=compiler_params,
    )(everything, left, left_other, gating, last_weights, vectors)


def solution(mesh):
    in_specs = (P(("groups", "row"), "col", None), P(), P(), P(), P(), P(), P(), P(), P(), P(), P())
    out_specs = P(("groups", "row"), "col", None)
    return jax.shard_map(
        on_device, mesh=mesh, in_specs=in_specs, out_specs=out_specs, check_vma=False
    )
```

```python
import functools

import jax
import jax.numpy as jnp
from jax import lax
from jax.experimental import pallas as pl
from jax.experimental.pallas import tpu as pltpu
from jax.sharding import PartitionSpec as P

GROUP = 16
TOKENS_AT_ONCE = 512
VMEM_LIMIT = 48 * 1024 * 1024


def layer_norm(values, norm_gain, norm_bias):
    average = jnp.mean(values, axis=-1, keepdims=True)
    centred = values - average
    variance = jnp.mean(centred * centred, axis=-1, keepdims=True)
    return centred * lax.rsqrt(variance + 1e-05) * norm_gain + norm_bias


def normed_of(blocks, gain, bias):
    values = jnp.concatenate(blocks, axis=0).astype(jnp.float32)
    return layer_norm(values, gain[...], bias[...]).astype(jnp.bfloat16)


def gated(normed, gate_w, w):
    gate = jnp.dot(normed, gate_w[...], preferred_element_type=jnp.float32)
    value = jnp.dot(normed, w[...], preferred_element_type=jnp.float32)
    return (jax.nn.sigmoid(gate) * value).astype(jnp.bfloat16).astype(jnp.float32)


def fetch(*refs):
    count = len(refs) // 2
    sources, targets, sems = refs[:count], refs[count : 2 * count], refs[2 * count]
    copies = [
        pltpu.make_async_copy(source, target, sems.at[number])
        for number, (source, target) in enumerate(zip(sources, targets))
    ]
    for copy in copies:
        copy.start()
    for copy in copies:
        copy.wait()


def join(own, other, joined):
    col = lax.axis_index("col")
    joined[col] = own[...]
    joined[1 - col] = other[...]


def gather(near, *refs):
    blocks, gathered = refs[:near], refs[near]
    place = lax.rem(lax.axis_index("row"), near)
    for turn in range(near):
        gathered[lax.bitwise_xor(place, turn)] = blocks[turn][...]


def own_rows(joined, in_gain, in_bias, left_gate_w, left_w, out_gate_w, left, gating):
    col_parts, rows, cols, channels = joined.shape
    blocks = [joined[part, a] for a in range(rows) for part in range(col_parts)]
    left[...] = gated(normed_of(blocks, in_gain, in_bias), left_gate_w, left_w)
    mine = joined[lax.axis_index("col")].reshape(rows * cols, channels)
    gate = jnp.dot(
        normed_of([mine], in_gain, in_bias), out_gate_w[...], preferred_element_type=jnp.float32
    )
    gating[...] = jax.nn.sigmoid(gate)


def triangle(owners, near, *refs):
    far = owners // near
    home_blocks, away_blocks = refs[:far], refs[far : 2 * far]
    left, gating, in_gain, in_bias, right_gate_w, right_w = refs[2 * far : 2 * far + 6]
    mid_gain, mid_bias, out_w, out, raw_held, right_held = refs[2 * far + 6 :]
    rows, cols, channels = out.shape
    col_parts = raw_held.shape[1]
    depth = cols * col_parts
    row = lax.axis_index("row")
    at_home = row // owners == lax.axis_index("col")
    here = lax.rem(row, owners) // near

    def hold(blocks):
        for turn in range(far):
            raw_held[pl.ds(lax.bitwise_xor(here, turn) * near, near)] = blocks[turn][...]

    pl.when(at_home)(lambda: hold(home_blocks))
    pl.when(jnp.logical_not(at_home))(lambda: hold(away_blocks))

    rows_at_once = max(1, min(GROUP, TOKENS_AT_ONCE // depth))

    def one_group(group):
        for first in range(0, GROUP, rows_at_once):
            blocks = [
                raw_held[group * (GROUP // rows) + j // rows, part, j % rows]
                for j in range(first, first + rows_at_once)
                for part in range(col_parts)
            ]
            right_held[first * depth : (first + rows_at_once) * depth] = gated(
                normed_of(blocks, in_gain, in_bias), right_gate_w, right_w
            )

        def add(k, sums):
            right = right_held[pl.ds(k, GROUP, stride=depth)]
            return [sums[a] + left[pl.ds(a * depth + k, 1)] * right for a in range(rows)]

        sums = [jnp.zeros((GROUP, right_held.shape[1]), jnp.float32)] * rows
        if depth <= 32:
            for k in range(depth):
                sums = add(k, sums)
        else:
            sums = lax.fori_loop(0, depth, add, sums, unroll=8)
        middle = layer_norm(jnp.concatenate(sums, axis=0), mid_gain[...], mid_bias[...])
        update = jnp.dot(
            middle.astype(jnp.bfloat16), out_w[...], preferred_element_type=jnp.float32
        )
        for a in range(rows):
            gate = gating[pl.ds(pl.multiple_of(a * cols + group * GROUP, 8), GROUP)]
            result = gate * update[a * GROUP : (a + 1) * GROUP]
            out[a, pl.ds(pl.multiple_of(group * GROUP, GROUP), GROUP)] = result.astype(out.dtype)

    groups = cols // GROUP
    if groups == 1:
        one_group(0)
    else:
        pl.loop(0, groups)(one_group)


def on_device(pair_repr, *params):
    rows, cols, channels = pair_repr.shape
    hidden = params[3].shape[1]
    row_parts, col_parts = lax.axis_size("row"), lax.axis_size("col")
    depth = cols * col_parts
    owners = cols // rows
    near = 1 << ((owners.bit_length() - 1) // 2)
    far = owners // near
    f32, bf16 = jnp.float32, jnp.bfloat16
    shape = jax.ShapeDtypeStruct
    vmem = pl.BlockSpec(memory_space=pltpu.VMEM)

    def call(body, name, outs, ins, scratch=(), in_spec=vmem):
        return pl.pallas_call(
            body,
            name=name,
            out_shape=outs,
            in_specs=[in_spec] * len(ins),
            out_specs=[vmem] * len(outs),
            scratch_shapes=list(scratch),
            compiler_params=pltpu.CompilerParams(vmem_limit_bytes=VMEM_LIMIT),
        )(*ins)

    other = lax.ppermute(pair_repr, "col", [(0, 1), (1, 0)])
    sources = [pair_repr] + [p.reshape(1, -1) if p.ndim == 1 else p for p in params]
    own, *params = call(
        fetch,
        "fetch",
        [shape(source.shape, source.dtype) for source in sources],
        [pltpu.with_memory_space_constraint(source, pltpu.HBM) for source in sources],
        [pltpu.SemaphoreType.DMA((len(sources),))],
        pl.BlockSpec(memory_space=pltpu.HBM),
    )
    (
        in_gain,
        in_bias,
        left_gate_w,
        left_w,
        right_gate_w,
        right_w,
        out_gate_w,
        mid_gain,
        mid_bias,
        out_w,
    ) = params
    (joined,) = call(join, "join", [shape((col_parts,) + pair_repr.shape, bf16)], [own, other])

    def device(half, place, away):
        return ((half + away) % 2 * owners + place) * col_parts + half

    def moves(turn, away):
        return [
            (device(half, place, 0), device(half, place ^ turn, away))
            for half in range(2)
            for place in range(owners)
        ]

    def send(values, turn, away):
        return lax.ppermute(values, ("row", "col"), moves(turn, away))

    blocks = [joined] + [send(joined, turn, 0) for turn in range(1, near)]
    (gathered,) = call(
        functools.partial(gather, near), "gather", [shape((near,) + joined.shape, bf16)], blocks
    )
    away_blocks = [send(gathered, turn * near, 1) for turn in range(far)]
    home_blocks = [gathered] + [send(gathered, turn * near, 0) for turn in range(1, far)]

    left, gating = call(
        own_rows,
        "own_rows",
        [shape((rows * depth, hidden), f32), shape((rows * cols, channels), f32)],
        [joined, in_gain, in_bias, left_gate_w, left_w, out_gate_w],
    )
    (update,) = call(
        functools.partial(triangle, owners, near),
        "triangle",
        [shape(pair_repr.shape, bf16)],
        home_blocks
        + away_blocks
        + [left, gating, in_gain, in_bias, right_gate_w, right_w, mid_gain, mid_bias, out_w],
        [
            pltpu.VMEM((owners, col_parts) + pair_repr.shape, bf16),
            pltpu.VMEM((GROUP * depth, hidden), f32),
        ],
    )
    return update


def solution(mesh):
    in_specs = (P(("groups", "row"), "col", None), P(), P(), P(), P(), P(), P(), P(), P(), P(), P())
    out_specs = P(("groups", "row"), "col", None)
    return jax.shard_map(
        on_device, mesh=mesh, in_specs=in_specs, out_specs=out_specs, check_vma=False
    )
```

```python
import functools

import jax
import jax.numpy as jnp
from jax import lax
from jax.experimental import pallas as pl
from jax.experimental.pallas import tpu as pltpu
from jax.sharding import PartitionSpec as P

GROUP = 16
TOKENS_AT_ONCE = 512
VMEM_LIMIT = 48 * 1024 * 1024


def layer_norm(values, norm_gain, norm_bias):
    average = jnp.mean(values, axis=-1, keepdims=True)
    centred = values - average
    variance = jnp.mean(centred * centred, axis=-1, keepdims=True)
    return centred * lax.rsqrt(variance + 1e-05) * norm_gain + norm_bias


def normed_of(blocks, gain, bias):
    values = jnp.concatenate(blocks, axis=0).astype(jnp.float32)
    return layer_norm(values, gain[...], bias[...]).astype(jnp.bfloat16)


def gated(normed, gate_w, w):
    gate = jnp.dot(normed, gate_w[...], preferred_element_type=jnp.float32)
    value = jnp.dot(normed, w[...], preferred_element_type=jnp.float32)
    return (jax.nn.sigmoid(gate) * value).astype(jnp.bfloat16).astype(jnp.float32)


def fetch(*refs):
    count = len(refs) // 2
    sources, targets, sems = refs[:count], refs[count : 2 * count], refs[2 * count]
    copies = [
        pltpu.make_async_copy(source, target, sems.at[number])
        for number, (source, target) in enumerate(zip(sources, targets))
    ]
    for copy in copies:
        copy.start()
    for copy in copies:
        copy.wait()


def join(own, other, joined):
    col = lax.axis_index("col")
    joined[col] = own[...]
    joined[1 - col] = other[...]


def choose(owners, joined, crossed, mine):
    at_home = lax.axis_index("row") // owners == lax.axis_index("col")

    @pl.when(at_home)
    def _():
        mine[...] = joined[...]

    @pl.when(jnp.logical_not(at_home))
    def _():
        mine[...] = crossed[...]


def own_rows(joined, in_gain, in_bias, left_gate_w, left_w, out_gate_w, left, gating):
    col_parts, rows, cols, channels = joined.shape
    blocks = [joined[part, a] for a in range(rows) for part in range(col_parts)]
    left[...] = gated(normed_of(blocks, in_gain, in_bias), left_gate_w, left_w)
    mine = joined[lax.axis_index("col")].reshape(rows * cols, channels)
    gate = jnp.dot(
        normed_of([mine], in_gain, in_bias), out_gate_w[...], preferred_element_type=jnp.float32
    )
    gating[...] = jax.nn.sigmoid(gate)


def triangle(owners, *refs):
    blocks = refs[:owners]
    left, gating, in_gain, in_bias, right_gate_w, right_w = refs[owners : owners + 6]
    mid_gain, mid_bias, out_w, out, raw_held, right_held = refs[owners + 6 :]
    rows, cols, channels = out.shape
    col_parts = raw_held.shape[1]
    depth = cols * col_parts
    place = lax.rem(lax.axis_index("row"), owners)
    for turn in range(owners):
        raw_held[lax.bitwise_xor(place, turn)] = blocks[turn][...]

    rows_at_once = max(1, min(GROUP, TOKENS_AT_ONCE // depth))

    def one_group(group):
        for first in range(0, GROUP, rows_at_once):
            blocks = [
                raw_held[group * (GROUP // rows) + j // rows, part, j % rows]
                for j in range(first, first + rows_at_once)
                for part in range(col_parts)
            ]
            right_held[first * depth : (first + rows_at_once) * depth] = gated(
                normed_of(blocks, in_gain, in_bias), right_gate_w, right_w
            )

        def add(k, sums):
            right = right_held[pl.ds(k, GROUP, stride=depth)]
            return [sums[a] + left[pl.ds(a * depth + k, 1)] * right for a in range(rows)]

        sums = [jnp.zeros((GROUP, right_held.shape[1]), jnp.float32)] * rows
        if depth <= 32:
            for k in range(depth):
                sums = add(k, sums)
        else:
            sums = lax.fori_loop(0, depth, add, sums, unroll=8)
        middle = layer_norm(jnp.concatenate(sums, axis=0), mid_gain[...], mid_bias[...])
        update = jnp.dot(
            middle.astype(jnp.bfloat16), out_w[...], preferred_element_type=jnp.float32
        )
        for a in range(rows):
            gate = gating[pl.ds(pl.multiple_of(a * cols + group * GROUP, 8), GROUP)]
            result = gate * update[a * GROUP : (a + 1) * GROUP]
            out[a, pl.ds(pl.multiple_of(group * GROUP, GROUP), GROUP)] = result.astype(out.dtype)

    groups = cols // GROUP
    if groups == 1:
        one_group(0)
    else:
        pl.loop(0, groups)(one_group)


def on_device(pair_repr, *params):
    rows, cols, channels = pair_repr.shape
    hidden = params[3].shape[1]
    row_parts, col_parts = lax.axis_size("row"), lax.axis_size("col")
    depth = cols * col_parts
    owners = cols // rows
    f32, bf16 = jnp.float32, jnp.bfloat16
    shape = jax.ShapeDtypeStruct
    vmem = pl.BlockSpec(memory_space=pltpu.VMEM)

    def call(body, name, outs, ins, scratch=(), in_spec=vmem):
        return pl.pallas_call(
            body,
            name=name,
            out_shape=outs,
            in_specs=[in_spec] * len(ins),
            out_specs=[vmem] * len(outs),
            scratch_shapes=list(scratch),
            compiler_params=pltpu.CompilerParams(vmem_limit_bytes=VMEM_LIMIT),
        )(*ins)

    other = lax.ppermute(pair_repr, "col", [(0, 1), (1, 0)])
    sources = [pair_repr] + [p.reshape(1, -1) if p.ndim == 1 else p for p in params]
    own, *params = call(
        fetch,
        "fetch",
        [shape(source.shape, source.dtype) for source in sources],
        [pltpu.with_memory_space_constraint(source, pltpu.HBM) for source in sources],
        [pltpu.SemaphoreType.DMA((len(sources),))],
        pl.BlockSpec(memory_space=pltpu.HBM),
    )
    (
        in_gain,
        in_bias,
        left_gate_w,
        left_w,
        right_gate_w,
        right_w,
        out_gate_w,
        mid_gain,
        mid_bias,
        out_w,
    ) = params
    (joined,) = call(join, "join", [shape((col_parts,) + pair_repr.shape, bf16)], [own, other])

    def swap(values, target):
        pairs = [
            (r * col_parts + c, target(r) * col_parts + c)
            for r in range(row_parts)
            for c in range(col_parts)
        ]
        return lax.ppermute(values, ("row", "col"), pairs)

    crossed = swap(joined, lambda r: (r + owners) % row_parts)
    (mine,) = call(
        functools.partial(choose, owners), "choose", [shape(joined.shape, bf16)], [joined, crossed]
    )
    blocks = [mine] + [swap(mine, lambda r, turn=turn: r ^ turn) for turn in range(1, owners)]

    left, gating = call(
        own_rows,
        "own_rows",
        [shape((rows * depth, hidden), f32), shape((rows * cols, channels), f32)],
        [joined, in_gain, in_bias, left_gate_w, left_w, out_gate_w],
    )
    (update,) = call(
        functools.partial(triangle, owners),
        "triangle",
        [shape(pair_repr.shape, bf16)],
        blocks
        + [left, gating, in_gain, in_bias, right_gate_w, right_w, mid_gain, mid_bias, out_w],
        [
            pltpu.VMEM((owners, col_parts) + pair_repr.shape, bf16),
            pltpu.VMEM((GROUP * depth, hidden), f32),
        ],
    )
    return update


def solution(mesh):
    in_specs = (P(("groups", "row"), "col", None), P(), P(), P(), P(), P(), P(), P(), P(), P(), P())
    out_specs = P(("groups", "row"), "col", None)
    return jax.shard_map(
        on_device, mesh=mesh, in_specs=in_specs, out_specs=out_specs, check_vma=False
    )
```

```python
import functools

import jax
import jax.numpy as jnp
from jax import lax
from jax.experimental import pallas as pl
from jax.experimental.pallas import tpu as pltpu
from jax.sharding import PartitionSpec as P

GROUP = 16
TOKENS_AT_ONCE = 512
VMEM_LIMIT = 48 * 1024 * 1024


def layer_norm(values, norm_gain, norm_bias):
    average = jnp.mean(values, axis=-1, keepdims=True)
    centred = values - average
    variance = jnp.mean(centred * centred, axis=-1, keepdims=True)
    return centred * lax.rsqrt(variance + 1e-05) * norm_gain + norm_bias


def normed_of(blocks, gain, bias):
    values = jnp.concatenate(blocks, axis=0).astype(jnp.float32)
    return layer_norm(values, gain[...], bias[...]).astype(jnp.bfloat16)


def gated(normed, gate_w, w):
    gate = jnp.dot(normed, gate_w[...], preferred_element_type=jnp.float32)
    value = jnp.dot(normed, w[...], preferred_element_type=jnp.float32)
    return (jax.nn.sigmoid(gate) * value).astype(jnp.bfloat16).astype(jnp.float32)


def fetch(*refs):
    count = len(refs) // 2
    sources, targets, sems = refs[:count], refs[count : 2 * count], refs[2 * count]
    copies = [
        pltpu.make_async_copy(source, target, sems.at[number])
        for number, (source, target) in enumerate(zip(sources, targets))
    ]
    for copy in copies:
        copy.start()
    for copy in copies:
        copy.wait()


def join(own, other, joined):
    col = lax.axis_index("col")
    joined[col] = own[...]
    joined[1 - col] = other[...]


def own_rows(joined, in_gain, in_bias, left_gate_w, left_w, out_gate_w, left, gating):
    col_parts, rows, cols, channels = joined.shape
    blocks = [joined[part, a] for a in range(rows) for part in range(col_parts)]
    left[...] = gated(normed_of(blocks, in_gain, in_bias), left_gate_w, left_w)
    mine = joined[lax.axis_index("col")].reshape(rows * cols, channels)
    gate = jnp.dot(
        normed_of([mine], in_gain, in_bias), out_gate_w[...], preferred_element_type=jnp.float32
    )
    gating[...] = jax.nn.sigmoid(gate)


def triangle(owners, *refs):
    blocks = refs[:owners]
    left, gating, in_gain, in_bias, right_gate_w, right_w = refs[owners : owners + 6]
    mid_gain, mid_bias, out_w, out, raw_held, right_held = refs[owners + 6 :]
    rows, cols, channels = out.shape
    col_parts = raw_held.shape[1]
    depth = cols * col_parts
    place = lax.rem(lax.axis_index("row"), owners)
    for turn in range(owners):
        raw_held[lax.bitwise_xor(place, turn)] = blocks[turn][...]

    rows_at_once = max(1, min(GROUP, TOKENS_AT_ONCE // depth))

    def one_group(group):
        for first in range(0, GROUP, rows_at_once):
            blocks = [
                raw_held[group * (GROUP // rows) + j // rows, part, j % rows]
                for j in range(first, first + rows_at_once)
                for part in range(col_parts)
            ]
            right_held[first * depth : (first + rows_at_once) * depth] = gated(
                normed_of(blocks, in_gain, in_bias), right_gate_w, right_w
            )

        def add(k, sums):
            right = right_held[pl.ds(k, GROUP, stride=depth)]
            return [sums[a] + left[pl.ds(a * depth + k, 1)] * right for a in range(rows)]

        sums = [jnp.zeros((GROUP, right_held.shape[1]), jnp.float32)] * rows
        if depth <= 32:
            for k in range(depth):
                sums = add(k, sums)
        else:
            sums = lax.fori_loop(0, depth, add, sums, unroll=8)
        middle = layer_norm(jnp.concatenate(sums, axis=0), mid_gain[...], mid_bias[...])
        update = jnp.dot(
            middle.astype(jnp.bfloat16), out_w[...], preferred_element_type=jnp.float32
        )
        for a in range(rows):
            gate = gating[pl.ds(pl.multiple_of(a * cols + group * GROUP, 8), GROUP)]
            result = gate * update[a * GROUP : (a + 1) * GROUP]
            out[a, pl.ds(pl.multiple_of(group * GROUP, GROUP), GROUP)] = result.astype(out.dtype)

    groups = cols // GROUP
    if groups == 1:
        one_group(0)
    else:
        pl.loop(0, groups)(one_group)


def on_device(pair_repr, *params):
    rows, cols, channels = pair_repr.shape
    hidden = params[3].shape[1]
    row_parts, col_parts = lax.axis_size("row"), lax.axis_size("col")
    depth = cols * col_parts
    owners = cols // rows
    f32, bf16 = jnp.float32, jnp.bfloat16
    shape = jax.ShapeDtypeStruct
    vmem = pl.BlockSpec(memory_space=pltpu.VMEM)

    def call(body, name, outs, ins, scratch=(), in_spec=vmem):
        return pl.pallas_call(
            body,
            name=name,
            out_shape=outs,
            in_specs=[in_spec] * len(ins),
            out_specs=[vmem] * len(outs),
            scratch_shapes=list(scratch),
            compiler_params=pltpu.CompilerParams(vmem_limit_bytes=VMEM_LIMIT),
        )(*ins)

    other = lax.ppermute(pair_repr, "col", [(0, 1), (1, 0)])
    sources = [pair_repr] + [p.reshape(1, -1) if p.ndim == 1 else p for p in params]
    own, *params = call(
        fetch,
        "fetch",
        [shape(source.shape, source.dtype) for source in sources],
        [pltpu.with_memory_space_constraint(source, pltpu.HBM) for source in sources],
        [pltpu.SemaphoreType.DMA((len(sources),))],
        pl.BlockSpec(memory_space=pltpu.HBM),
    )
    (
        in_gain,
        in_bias,
        left_gate_w,
        left_w,
        right_gate_w,
        right_w,
        out_gate_w,
        mid_gain,
        mid_bias,
        out_w,
    ) = params
    (joined,) = call(join, "join", [shape((col_parts,) + pair_repr.shape, bf16)], [own, other])

    across, swaps = [], [[] for _ in range(owners)]
    for r in range(row_parts):
        half = r // owners
        home, away = r * col_parts + half, r * col_parts + 1 - half
        across += [(home, (r + owners) % row_parts * col_parts + half), (away, home)]
        for turn in range(1, owners):
            swaps[turn] += [(r * col_parts + c, (r ^ turn) * col_parts + c) for c in range(2)]
    mine = lax.ppermute(joined, ("row", "col"), across)
    blocks = [mine] + [lax.ppermute(mine, ("row", "col"), pairs) for pairs in swaps[1:]]

    left, gating = call(
        own_rows,
        "own_rows",
        [shape((rows * depth, hidden), f32), shape((rows * cols, channels), f32)],
        [joined, in_gain, in_bias, left_gate_w, left_w, out_gate_w],
    )
    (update,) = call(
        functools.partial(triangle, owners),
        "triangle",
        [shape(pair_repr.shape, bf16)],
        blocks
        + [left, gating, in_gain, in_bias, right_gate_w, right_w, mid_gain, mid_bias, out_w],
        [
            pltpu.VMEM((owners, col_parts) + pair_repr.shape, bf16),
            pltpu.VMEM((GROUP * depth, hidden), f32),
        ],
    )
    return update


def solution(mesh):
    in_specs = (P(("groups", "row"), "col", None), P(), P(), P(), P(), P(), P(), P(), P(), P(), P())
    out_specs = P(("groups", "row"), "col", None)
    return jax.shard_map(
        on_device, mesh=mesh, in_specs=in_specs, out_specs=out_specs, check_vma=False
    )
```

```python
import functools

import jax
import jax.numpy as jnp
from jax import lax
from jax.experimental import pallas as pl
from jax.experimental.pallas import tpu as pltpu
from jax.sharding import PartitionSpec as P

GROUP = 16
TOKENS_AT_ONCE = 512
VMEM_LIMIT = 48 * 1024 * 1024


def layer_norm(values, norm_gain, norm_bias):
    average = jnp.mean(values, axis=-1, keepdims=True)
    centred = values - average
    variance = jnp.mean(centred * centred, axis=-1, keepdims=True)
    return centred * lax.rsqrt(variance + 1e-05) * norm_gain + norm_bias


def normed_of(blocks, gain, bias):
    values = jnp.concatenate(blocks, axis=0).astype(jnp.float32)
    return layer_norm(values, gain[...], bias[...]).astype(jnp.bfloat16)


def gated(normed, gate_w, w):
    gate = jnp.dot(normed, gate_w[...], preferred_element_type=jnp.float32)
    value = jnp.dot(normed, w[...], preferred_element_type=jnp.float32)
    return (jax.nn.sigmoid(gate) * value).astype(jnp.bfloat16).astype(jnp.float32)


def fetch(*refs):
    count = len(refs) // 2
    sources, targets, sems = refs[:count], refs[count : 2 * count], refs[2 * count]
    copies = [
        pltpu.make_async_copy(source, target, sems.at[number])
        for number, (source, target) in enumerate(zip(sources, targets))
    ]
    for copy in copies:
        copy.start()
    for copy in copies:
        copy.wait()


def join(own, other, joined):
    col = lax.axis_index("col")
    joined[col] = own[...]
    joined[1 - col] = other[...]


def merge(bit, held, received, merged):
    count = held.shape[0]
    side = lax.axis_index("row") >> bit & 1
    merged[pl.ds(side * count, count)] = held[...]
    merged[pl.ds((1 - side) * count, count)] = received[...]


def own_rows(joined, in_gain, in_bias, left_gate_w, left_w, out_gate_w, left, gating):
    col_parts, rows, cols, channels = joined.shape
    blocks = [joined[part, a] for a in range(rows) for part in range(col_parts)]
    left[...] = gated(normed_of(blocks, in_gain, in_bias), left_gate_w, left_w)
    mine = joined[lax.axis_index("col")].reshape(rows * cols, channels)
    gate = jnp.dot(
        normed_of([mine], in_gain, in_bias), out_gate_w[...], preferred_element_type=jnp.float32
    )
    gating[...] = jax.nn.sigmoid(gate)


def update_columns(blocks, left, gating, params, right_held, column, target, first):
    in_gain, in_bias, right_gate_w, right_w, mid_gain, mid_bias, out_w = params
    places, col_parts, rows, cols, channels = blocks.shape
    depth = cols * col_parts
    group = min(GROUP, places * rows)
    rows_at_once = max(1, min(group, TOKENS_AT_ONCE // depth))

    def one_group(number):
        for begin in range(0, group, rows_at_once):
            some = [
                blocks[number * (group // rows) + j // rows, part, j % rows]
                for j in range(begin, begin + rows_at_once)
                for part in range(col_parts)
            ]
            right_held[begin * depth : (begin + rows_at_once) * depth] = gated(
                normed_of(some, in_gain, in_bias), right_gate_w, right_w
            )

        def add(k, sums):
            right = right_held[pl.ds(k, group, stride=depth)]
            return [sums[a] + left[pl.ds(a * depth + k, 1)] * right for a in range(rows)]

        sums = [jnp.zeros((group, right_held.shape[1]), jnp.float32)] * rows
        if depth <= 32:
            for k in range(depth):
                sums = add(k, sums)
        else:
            sums = lax.fori_loop(0, depth, add, sums, unroll=8)
        middle = layer_norm(jnp.concatenate(sums, axis=0), mid_gain[...], mid_bias[...])
        update = jnp.dot(
            middle.astype(jnp.bfloat16), out_w[...], preferred_element_type=jnp.float32
        )
        for a in range(rows):
            at = pl.multiple_of(a * cols + column + number * group, 8)
            into = pl.multiple_of(first + number * group, 8)
            target[a, pl.ds(into, group)] = (
                gating[pl.ds(at, group)] * update[a * group : (a + 1) * group]
            )

    groups = places * rows // group
    if groups == 1:
        one_group(0)
    else:
        pl.loop(0, groups)(one_group)


def first_columns(bit, blocks, left, gating, *refs):
    params, part, right_held = refs[:7], refs[7], refs[8]
    column = (lax.axis_index("row") >> bit & 1) * part.shape[1]
    update_columns(blocks, left, gating, params, right_held, column, part, 0)


def last_columns(bit, blocks, part, left, gating, *refs):
    params, out, right_held, whole = refs[:7], refs[7], refs[8], refs[9]
    count = part.shape[1]
    side = lax.axis_index("row") >> bit & 1
    column = (1 - side) * count
    update_columns(blocks, left, gating, params, right_held, column, whole, column)
    whole[:, pl.ds(pl.multiple_of(side * count, 8), count)] = part[...]
    out[...] = whole[...].astype(out.dtype)


def on_device(pair_repr, *params):
    rows, cols, channels = pair_repr.shape
    hidden = params[3].shape[1]
    row_parts, col_parts = lax.axis_size("row"), lax.axis_size("col")
    depth = cols * col_parts
    owners = cols // rows
    f32, bf16 = jnp.float32, jnp.bfloat16
    shape = jax.ShapeDtypeStruct
    vmem = pl.BlockSpec(memory_space=pltpu.VMEM)

    def call(body, name, outs, ins, scratch=(), in_spec=vmem):
        return pl.pallas_call(
            body,
            name=name,
            out_shape=outs,
            in_specs=[in_spec] * len(ins),
            out_specs=[vmem] * len(outs),
            scratch_shapes=list(scratch),
            compiler_params=pltpu.CompilerParams(vmem_limit_bytes=VMEM_LIMIT),
        )(*ins)

    other = lax.ppermute(pair_repr, "col", [(0, 1), (1, 0)])
    sources = [pair_repr] + [p.reshape(1, -1) if p.ndim == 1 else p for p in params]
    own, *params = call(
        fetch,
        "fetch",
        [shape(source.shape, source.dtype) for source in sources],
        [pltpu.with_memory_space_constraint(source, pltpu.HBM) for source in sources],
        [pltpu.SemaphoreType.DMA((len(sources),))],
        pl.BlockSpec(memory_space=pltpu.HBM),
    )
    (
        in_gain,
        in_bias,
        left_gate_w,
        left_w,
        right_gate_w,
        right_w,
        out_gate_w,
        mid_gain,
        mid_bias,
        out_w,
    ) = params
    (joined,) = call(join, "join", [shape((col_parts,) + pair_repr.shape, bf16)], [own, other])

    across = []
    for r in range(row_parts):
        half = r // owners
        home, away = r * col_parts + half, r * col_parts + 1 - half
        across += [(home, (r + owners) % row_parts * col_parts + half), (away, home)]
    held = lax.ppermute(joined, ("row", "col"), across)[None]
    last = owners.bit_length() - 2
    for bit in range(last + 1):
        pairs = [(r, r ^ 1 << bit) for r in range(row_parts)]
        received = lax.ppermute(held, "row", pairs)
        if bit < last:
            merged = shape((2 * held.shape[0],) + joined.shape, bf16)
            (held,) = call(functools.partial(merge, bit), "merge", [merged], [held, received])

    left, gating = call(
        own_rows,
        "own_rows",
        [shape((rows * depth, hidden), f32), shape((rows * cols, channels), f32)],
        [joined, in_gain, in_bias, left_gate_w, left_w, out_gate_w],
    )
    shared = [left, gating, in_gain, in_bias, right_gate_w, right_w, mid_gain, mid_bias, out_w]
    count = held.shape[0] * rows
    right_held = pltpu.VMEM((min(GROUP, count) * depth, hidden), f32)
    (part,) = call(
        functools.partial(first_columns, last),
        "first_columns",
        [shape((rows, count, channels), f32)],
        [held] + shared,
        [right_held],
    )
    (update,) = call(
        functools.partial(last_columns, last),
        "last_columns",
        [shape(pair_repr.shape, bf16)],
        [received, part] + shared,
        [right_held, pltpu.VMEM(pair_repr.shape, f32)],
    )
    return update


def solution(mesh):
    in_specs = (P(("groups", "row"), "col", None), P(), P(), P(), P(), P(), P(), P(), P(), P(), P())
    out_specs = P(("groups", "row"), "col", None)
    return jax.shard_map(
        on_device, mesh=mesh, in_specs=in_specs, out_specs=out_specs, check_vma=False
    )
```

```python
import functools

import jax
import jax.numpy as jnp
from jax import lax
from jax.experimental import pallas as pl
from jax.experimental.pallas import tpu as pltpu
from jax.sharding import PartitionSpec as P

GROUP = 16
TOKENS_AT_ONCE = 512
VMEM_LIMIT = 48 * 1024 * 1024


def layer_norm(values, norm_gain, norm_bias):
    average = jnp.mean(values, axis=-1, keepdims=True)
    centred = values - average
    variance = jnp.mean(centred * centred, axis=-1, keepdims=True)
    return centred * lax.rsqrt(variance + 1e-05) * norm_gain + norm_bias


def normed_of(blocks, gain, bias):
    values = jnp.concatenate(blocks, axis=0).astype(jnp.float32)
    return layer_norm(values, gain[...], bias[...]).astype(jnp.bfloat16)


def gated(normed, gate_w, w):
    gate = jnp.dot(normed, gate_w[...], preferred_element_type=jnp.float32)
    value = jnp.dot(normed, w[...], preferred_element_type=jnp.float32)
    return (jax.nn.sigmoid(gate) * value).astype(jnp.bfloat16).astype(jnp.float32)


def fetch(*refs):
    count = len(refs) // 2
    sources, targets, sems = refs[:count], refs[count : 2 * count], refs[2 * count]
    copies = [
        pltpu.make_async_copy(source, target, sems.at[number])
        for number, (source, target) in enumerate(zip(sources, targets))
    ]
    for copy in copies:
        copy.start()
    for copy in copies:
        copy.wait()


def join(own, other, joined):
    col = lax.axis_index("col")
    joined[col] = own[...]
    joined[1 - col] = other[...]


def own_rows(joined, in_gain, in_bias, left_gate_w, left_w, out_gate_w, left, gating):
    col_parts, rows, cols, channels = joined.shape
    blocks = [joined[part, a] for a in range(rows) for part in range(col_parts)]
    left[...] = gated(normed_of(blocks, in_gain, in_bias), left_gate_w, left_w)
    mine = joined[lax.axis_index("col")].reshape(rows * cols, channels)
    gate = jnp.dot(
        normed_of([mine], in_gain, in_bias), out_gate_w[...], preferred_element_type=jnp.float32
    )
    gating[...] = jax.nn.sigmoid(gate)


def triangle(owners, *refs):
    blocks = refs[:owners]
    left, gating, in_gain, in_bias, right_gate_w, right_w = refs[owners : owners + 6]
    mid_gain, mid_bias, out_w, out, raw_held, right_held = refs[owners + 6 :]
    rows, cols, channels = out.shape
    col_parts = raw_held.shape[1]
    depth = cols * col_parts
    place = lax.rem(lax.axis_index("row"), owners)
    for turn in range(owners):
        raw_held[lax.bitwise_xor(place, turn)] = blocks[turn][...]

    rows_at_once = max(1, min(GROUP, TOKENS_AT_ONCE // depth))

    def one_group(group):
        for first in range(0, GROUP, rows_at_once):
            blocks = [
                raw_held[group * (GROUP // rows) + j // rows, part, j % rows]
                for j in range(first, first + rows_at_once)
                for part in range(col_parts)
            ]
            right_held[first * depth : (first + rows_at_once) * depth] = gated(
                normed_of(blocks, in_gain, in_bias), right_gate_w, right_w
            )

        def add(k, sums):
            right = right_held[pl.ds(k, GROUP, stride=depth)]
            return [sums[a] + left[pl.ds(a * depth + k, 1)] * right for a in range(rows)]

        sums = [jnp.zeros((GROUP, right_held.shape[1]), jnp.float32)] * rows
        if depth <= 32:
            for k in range(depth):
                sums = add(k, sums)
        else:
            sums = lax.fori_loop(0, depth, add, sums, unroll=8)
        middle = layer_norm(jnp.concatenate(sums, axis=0), mid_gain[...], mid_bias[...])
        update = jnp.dot(
            middle.astype(jnp.bfloat16), out_w[...], preferred_element_type=jnp.float32
        )
        for a in range(rows):
            gate = gating[pl.ds(pl.multiple_of(a * cols + group * GROUP, 8), GROUP)]
            result = gate * update[a * GROUP : (a + 1) * GROUP]
            out[a, pl.ds(pl.multiple_of(group * GROUP, GROUP), GROUP)] = result.astype(out.dtype)

    groups = cols // GROUP
    if groups == 1:
        one_group(0)
    else:
        pl.loop(0, groups)(one_group)


def on_device(pair_repr, *params):
    rows, cols, channels = pair_repr.shape
    hidden = params[3].shape[1]
    row_parts, col_parts = lax.axis_size("row"), lax.axis_size("col")
    depth = cols * col_parts
    owners = cols // rows
    f32, bf16 = jnp.float32, jnp.bfloat16
    shape = jax.ShapeDtypeStruct
    vmem = pl.BlockSpec(memory_space=pltpu.VMEM)

    def call(body, name, outs, ins, scratch=(), in_spec=vmem):
        return pl.pallas_call(
            body,
            name=name,
            out_shape=outs,
            in_specs=[in_spec] * len(ins),
            out_specs=[vmem] * len(outs),
            scratch_shapes=list(scratch),
            compiler_params=pltpu.CompilerParams(vmem_limit_bytes=VMEM_LIMIT),
        )(*ins)

    other = lax.ppermute(pair_repr, "col", [(0, 1), (1, 0)])
    sources = [pair_repr] + [p.reshape(1, -1) if p.ndim == 1 else p for p in params]
    own, *params = call(
        fetch,
        "fetch",
        [shape(source.shape, source.dtype) for source in sources],
        [pltpu.with_memory_space_constraint(source, pltpu.HBM) for source in sources],
        [pltpu.SemaphoreType.DMA((len(sources),))],
        pl.BlockSpec(memory_space=pltpu.HBM),
    )
    (
        in_gain,
        in_bias,
        left_gate_w,
        left_w,
        right_gate_w,
        right_w,
        out_gate_w,
        mid_gain,
        mid_bias,
        out_w,
    ) = params
    (joined,) = call(join, "join", [shape((col_parts,) + pair_repr.shape, bf16)], [own, other])

    blocks = []
    for turn in range(owners):
        pairs = []
        for r in range(row_parts):
            half = r // owners
            near = (r ^ turn) * col_parts + half
            far = (r ^ owners ^ turn) * col_parts + half
            pairs += [(r * col_parts + half, far), (r * col_parts + 1 - half, near)]
        blocks.append(lax.ppermute(joined, ("row", "col"), pairs))

    left, gating = call(
        own_rows,
        "own_rows",
        [shape((rows * depth, hidden), f32), shape((rows * cols, channels), f32)],
        [joined, in_gain, in_bias, left_gate_w, left_w, out_gate_w],
    )
    (update,) = call(
        functools.partial(triangle, owners),
        "triangle",
        [shape(pair_repr.shape, bf16)],
        blocks
        + [left, gating, in_gain, in_bias, right_gate_w, right_w, mid_gain, mid_bias, out_w],
        [
            pltpu.VMEM((owners, col_parts) + pair_repr.shape, bf16),
            pltpu.VMEM((GROUP * depth, hidden), f32),
        ],
    )
    return update


def solution(mesh):
    in_specs = (P(("groups", "row"), "col", None), P(), P(), P(), P(), P(), P(), P(), P(), P(), P())
    out_specs = P(("groups", "row"), "col", None)
    return jax.shard_map(
        on_device, mesh=mesh, in_specs=in_specs, out_specs=out_specs, check_vma=False
    )
```

```python
import functools

import jax
import jax.numpy as jnp
from jax import lax
from jax.experimental import pallas as pl
from jax.experimental.pallas import tpu as pltpu
from jax.sharding import PartitionSpec as P

GROUP = 16
TOKENS_AT_ONCE = 512
VMEM_LIMIT = 48 * 1024 * 1024


FOUR_PLACES = (
    ((2, 3, True), (0, 2, False), (1, 0, True), (3, 1, False)),
    ((3, 0, True), (2, 1, False), (1, 2, True), (0, 3, False)),
)


def plan(owners):
    if owners == 4:
        return FOUR_PLACES
    return (tuple((turn, turn, True) for turn in reversed(range(owners))),) * 2


def layer_norm(values, norm_gain, norm_bias):
    average = jnp.mean(values, axis=-1, keepdims=True)
    centred = values - average
    variance = jnp.mean(centred * centred, axis=-1, keepdims=True)
    return centred * lax.rsqrt(variance + 1e-05) * norm_gain + norm_bias


def normed_of(blocks, gain, bias):
    values = jnp.concatenate(blocks, axis=0).astype(jnp.float32)
    return layer_norm(values, gain[...], bias[...]).astype(jnp.bfloat16)


def gated(normed, gate_w, w):
    gate = jnp.dot(normed, gate_w[...], preferred_element_type=jnp.float32)
    value = jnp.dot(normed, w[...], preferred_element_type=jnp.float32)
    return (jax.nn.sigmoid(gate) * value).astype(jnp.bfloat16).astype(jnp.float32)


def fetch(*refs):
    count = len(refs) // 2
    sources, targets, sems = refs[:count], refs[count : 2 * count], refs[2 * count]
    copies = [
        pltpu.make_async_copy(source, target, sems.at[number])
        for number, (source, target) in enumerate(zip(sources, targets))
    ]
    for copy in copies:
        copy.start()
    for copy in copies:
        copy.wait()


def join(own, other, joined):
    col = lax.axis_index("col")
    joined[col] = own[...]
    joined[1 - col] = other[...]


def own_rows(joined, in_gain, in_bias, left_gate_w, left_w, out_gate_w, left, gating):
    col_parts, rows, cols, channels = joined.shape
    blocks = [joined[part, a] for a in range(rows) for part in range(col_parts)]
    left[...] = gated(normed_of(blocks, in_gain, in_bias), left_gate_w, left_w)
    mine = joined[lax.axis_index("col")].reshape(rows * cols, channels)
    gate = jnp.dot(
        normed_of([mine], in_gain, in_bias), out_gate_w[...], preferred_element_type=jnp.float32
    )
    gating[...] = jax.nn.sigmoid(gate)


def triangle(owners, *refs):
    blocks = refs[:owners]
    left, gating, in_gain, in_bias, right_gate_w, right_w = refs[owners : owners + 6]
    mid_gain, mid_bias, out_w, out, raw_held, right_held = refs[owners + 6 :]
    rows, cols, channels = out.shape
    col_parts = raw_held.shape[1]
    depth = cols * col_parts
    row, col = lax.axis_index("row"), lax.axis_index("col")
    at_home = row // owners == col
    for block, (first, second) in zip(blocks, zip(*plan(owners))):
        turn = jnp.where(
            at_home,
            jnp.where(col == 0, first[1], second[1]),
            jnp.where(col == 0, first[0], second[0]),
        )
        raw_held[lax.bitwise_xor(lax.rem(row, owners), turn)] = block[...]

    rows_at_once = max(1, min(GROUP, TOKENS_AT_ONCE // depth))

    def one_group(group):
        for first in range(0, GROUP, rows_at_once):
            blocks = [
                raw_held[group * (GROUP // rows) + j // rows, part, j % rows]
                for j in range(first, first + rows_at_once)
                for part in range(col_parts)
            ]
            right_held[first * depth : (first + rows_at_once) * depth] = gated(
                normed_of(blocks, in_gain, in_bias), right_gate_w, right_w
            )

        def add(k, sums):
            right = right_held[pl.ds(k, GROUP, stride=depth)]
            return [sums[a] + left[pl.ds(a * depth + k, 1)] * right for a in range(rows)]

        sums = [jnp.zeros((GROUP, right_held.shape[1]), jnp.float32)] * rows
        if depth <= 32:
            for k in range(depth):
                sums = add(k, sums)
        else:
            sums = lax.fori_loop(0, depth, add, sums, unroll=8)
        middle = layer_norm(jnp.concatenate(sums, axis=0), mid_gain[...], mid_bias[...])
        update = jnp.dot(
            middle.astype(jnp.bfloat16), out_w[...], preferred_element_type=jnp.float32
        )
        for a in range(rows):
            gate = gating[pl.ds(pl.multiple_of(a * cols + group * GROUP, 8), GROUP)]
            result = gate * update[a * GROUP : (a + 1) * GROUP]
            out[a, pl.ds(pl.multiple_of(group * GROUP, GROUP), GROUP)] = result.astype(out.dtype)

    groups = cols // GROUP
    if groups == 1:
        one_group(0)
    else:
        pl.loop(0, groups)(one_group)


def on_device(pair_repr, *params):
    rows, cols, channels = pair_repr.shape
    hidden = params[3].shape[1]
    row_parts, col_parts = lax.axis_size("row"), lax.axis_size("col")
    depth = cols * col_parts
    owners = cols // rows
    f32, bf16 = jnp.float32, jnp.bfloat16
    shape = jax.ShapeDtypeStruct
    vmem = pl.BlockSpec(memory_space=pltpu.VMEM)

    def call(body, name, outs, ins, scratch=(), in_spec=vmem):
        return pl.pallas_call(
            body,
            name=name,
            out_shape=outs,
            in_specs=[in_spec] * len(ins),
            out_specs=[vmem] * len(outs),
            scratch_shapes=list(scratch),
            compiler_params=pltpu.CompilerParams(vmem_limit_bytes=VMEM_LIMIT),
        )(*ins)

    other = lax.ppermute(pair_repr, "col", [(0, 1), (1, 0)])
    sources = [pair_repr] + [p.reshape(1, -1) if p.ndim == 1 else p for p in params]
    own, *params = call(
        fetch,
        "fetch",
        [shape(source.shape, source.dtype) for source in sources],
        [pltpu.with_memory_space_constraint(source, pltpu.HBM) for source in sources],
        [pltpu.SemaphoreType.DMA((len(sources),))],
        pl.BlockSpec(memory_space=pltpu.HBM),
    )
    (
        in_gain,
        in_bias,
        left_gate_w,
        left_w,
        right_gate_w,
        right_w,
        out_gate_w,
        mid_gain,
        mid_bias,
        out_w,
    ) = params
    (joined,) = call(join, "join", [shape((col_parts,) + pair_repr.shape, bf16)], [own, other])

    blocks = []
    for step in reversed(range(owners)):
        pairs = []
        for r in range(row_parts):
            half = r // owners
            far_turn, near_turn, home_sends_far = plan(owners)[half][step]
            far = (r ^ owners ^ far_turn) * col_parts + half
            near = (r ^ near_turn) * col_parts + half
            home, away = r * col_parts + half, r * col_parts + 1 - half
            pairs += [(home, far), (away, near)] if home_sends_far else [(home, near), (away, far)]
        blocks.insert(0, lax.ppermute(joined, ("row", "col"), pairs))

    left, gating = call(
        own_rows,
        "own_rows",
        [shape((rows * depth, hidden), f32), shape((rows * cols, channels), f32)],
        [joined, in_gain, in_bias, left_gate_w, left_w, out_gate_w],
    )
    (update,) = call(
        functools.partial(triangle, owners),
        "triangle",
        [shape(pair_repr.shape, bf16)],
        blocks
        + [left, gating, in_gain, in_bias, right_gate_w, right_w, mid_gain, mid_bias, out_w],
        [
            pltpu.VMEM((owners, col_parts) + pair_repr.shape, bf16),
            pltpu.VMEM((GROUP * depth, hidden), f32),
        ],
    )
    return update


def solution(mesh):
    in_specs = (P(("groups", "row"), "col", None), P(), P(), P(), P(), P(), P(), P(), P(), P(), P())
    out_specs = P(("groups", "row"), "col", None)
    return jax.shard_map(
        on_device, mesh=mesh, in_specs=in_specs, out_specs=out_specs, check_vma=False
    )
```

```python
import functools

import jax
import jax.numpy as jnp
from jax import lax
from jax.experimental import pallas as pl
from jax.experimental.pallas import tpu as pltpu
from jax.sharding import PartitionSpec as P

GROUP = 16
TOKENS_AT_ONCE = 512
VMEM_LIMIT = 48 * 1024 * 1024


FOUR_PLACES = (
    ((2, 3), (1, 2), (0, 0), (3, 1)),
    ((1, 0), (3, 1), (2, 2), (0, 3)),
)


def plan(owners):
    if owners == 4:
        return FOUR_PLACES
    return (tuple((turn, turn) for turn in reversed(range(owners))),) * 2


def layer_norm(values, norm_gain, norm_bias):
    average = jnp.mean(values, axis=-1, keepdims=True)
    centred = values - average
    variance = jnp.mean(centred * centred, axis=-1, keepdims=True)
    return centred * lax.rsqrt(variance + 1e-05) * norm_gain + norm_bias


def normed_of(blocks, gain, bias):
    values = jnp.concatenate(blocks, axis=0).astype(jnp.float32)
    return layer_norm(values, gain[...], bias[...]).astype(jnp.bfloat16)


def gated(normed, gate_w, w):
    gate = jnp.dot(normed, gate_w[...], preferred_element_type=jnp.float32)
    value = jnp.dot(normed, w[...], preferred_element_type=jnp.float32)
    return (jax.nn.sigmoid(gate) * value).astype(jnp.bfloat16).astype(jnp.float32)


def fetch(*refs):
    count = len(refs) // 2
    sources, targets, sems = refs[:count], refs[count : 2 * count], refs[2 * count]
    copies = [
        pltpu.make_async_copy(source, target, sems.at[number])
        for number, (source, target) in enumerate(zip(sources, targets))
    ]
    for copy in copies:
        copy.start()
    for copy in copies:
        copy.wait()


def join(own, other, joined):
    col = lax.axis_index("col")
    joined[col] = own[...]
    joined[1 - col] = other[...]


def own_rows(joined, in_gain, in_bias, left_gate_w, left_w, out_gate_w, left, gating):
    col_parts, rows, cols, channels = joined.shape
    blocks = [joined[part, a] for a in range(rows) for part in range(col_parts)]
    left[...] = gated(normed_of(blocks, in_gain, in_bias), left_gate_w, left_w)
    mine = joined[lax.axis_index("col")].reshape(rows * cols, channels)
    gate = jnp.dot(
        normed_of([mine], in_gain, in_bias), out_gate_w[...], preferred_element_type=jnp.float32
    )
    gating[...] = jax.nn.sigmoid(gate)


def triangle(owners, *refs):
    blocks = refs[:owners]
    left, gating, in_gain, in_bias, right_gate_w, right_w = refs[owners : owners + 6]
    mid_gain, mid_bias, out_w, out, raw_held, right_held = refs[owners + 6 :]
    rows, cols, channels = out.shape
    col_parts = raw_held.shape[1]
    depth = cols * col_parts
    row, col = lax.axis_index("row"), lax.axis_index("col")
    at_home = row // owners == col
    for block, (first, second) in zip(blocks, zip(*plan(owners))):
        turn = jnp.where(
            at_home,
            jnp.where(col == 0, first[1], second[1]),
            jnp.where(col == 0, first[0], second[0]),
        )
        raw_held[lax.bitwise_xor(lax.rem(row, owners), turn)] = block[...]

    rows_at_once = max(1, min(GROUP, TOKENS_AT_ONCE // depth))

    def one_group(group):
        for first in range(0, GROUP, rows_at_once):
            blocks = [
                raw_held[group * (GROUP // rows) + j // rows, part, j % rows]
                for j in range(first, first + rows_at_once)
                for part in range(col_parts)
            ]
            right_held[first * depth : (first + rows_at_once) * depth] = gated(
                normed_of(blocks, in_gain, in_bias), right_gate_w, right_w
            )

        def add(k, sums):
            right = right_held[pl.ds(k, GROUP, stride=depth)]
            return [sums[a] + left[pl.ds(a * depth + k, 1)] * right for a in range(rows)]

        sums = [jnp.zeros((GROUP, right_held.shape[1]), jnp.float32)] * rows
        if depth <= 32:
            for k in range(depth):
                sums = add(k, sums)
        else:
            sums = lax.fori_loop(0, depth, add, sums, unroll=8)
        middle = layer_norm(jnp.concatenate(sums, axis=0), mid_gain[...], mid_bias[...])
        update = jnp.dot(
            middle.astype(jnp.bfloat16), out_w[...], preferred_element_type=jnp.float32
        )
        for a in range(rows):
            gate = gating[pl.ds(pl.multiple_of(a * cols + group * GROUP, 8), GROUP)]
            result = gate * update[a * GROUP : (a + 1) * GROUP]
            out[a, pl.ds(pl.multiple_of(group * GROUP, GROUP), GROUP)] = result.astype(out.dtype)

    groups = cols // GROUP
    if groups == 1:
        one_group(0)
    else:
        pl.loop(0, groups)(one_group)


def on_device(pair_repr, *params):
    rows, cols, channels = pair_repr.shape
    hidden = params[3].shape[1]
    row_parts, col_parts = lax.axis_size("row"), lax.axis_size("col")
    depth = cols * col_parts
    owners = cols // rows
    f32, bf16 = jnp.float32, jnp.bfloat16
    shape = jax.ShapeDtypeStruct
    vmem = pl.BlockSpec(memory_space=pltpu.VMEM)

    def call(body, name, outs, ins, scratch=(), in_spec=vmem):
        return pl.pallas_call(
            body,
            name=name,
            out_shape=outs,
            in_specs=[in_spec] * len(ins),
            out_specs=[vmem] * len(outs),
            scratch_shapes=list(scratch),
            compiler_params=pltpu.CompilerParams(vmem_limit_bytes=VMEM_LIMIT),
        )(*ins)

    other = lax.ppermute(pair_repr, "col", [(0, 1), (1, 0)])
    sources = [pair_repr] + [p.reshape(1, -1) if p.ndim == 1 else p for p in params]
    own, *params = call(
        fetch,
        "fetch",
        [shape(source.shape, source.dtype) for source in sources],
        [pltpu.with_memory_space_constraint(source, pltpu.HBM) for source in sources],
        [pltpu.SemaphoreType.DMA((len(sources),))],
        pl.BlockSpec(memory_space=pltpu.HBM),
    )
    (
        in_gain,
        in_bias,
        left_gate_w,
        left_w,
        right_gate_w,
        right_w,
        out_gate_w,
        mid_gain,
        mid_bias,
        out_w,
    ) = params
    (joined,) = call(join, "join", [shape((col_parts,) + pair_repr.shape, bf16)], [own, other])

    blocks = []
    for step in reversed(range(owners)):
        pairs = []
        for r in range(row_parts):
            half = r // owners
            far_turn, near_turn = plan(owners)[half][step]
            far = (r ^ owners ^ far_turn) * col_parts + half
            near = (r ^ near_turn) * col_parts + half
            pairs += [(r * col_parts + half, far), (r * col_parts + 1 - half, near)]
        blocks.insert(0, lax.ppermute(joined, ("row", "col"), pairs))

    left, gating = call(
        own_rows,
        "own_rows",
        [shape((rows * depth, hidden), f32), shape((rows * cols, channels), f32)],
        [joined, in_gain, in_bias, left_gate_w, left_w, out_gate_w],
    )
    (update,) = call(
        functools.partial(triangle, owners),
        "triangle",
        [shape(pair_repr.shape, bf16)],
        blocks
        + [left, gating, in_gain, in_bias, right_gate_w, right_w, mid_gain, mid_bias, out_w],
        [
            pltpu.VMEM((owners, col_parts) + pair_repr.shape, bf16),
            pltpu.VMEM((GROUP * depth, hidden), f32),
        ],
    )
    return update


def solution(mesh):
    in_specs = (P(("groups", "row"), "col", None), P(), P(), P(), P(), P(), P(), P(), P(), P(), P())
    out_specs = P(("groups", "row"), "col", None)
    return jax.shard_map(
        on_device, mesh=mesh, in_specs=in_specs, out_specs=out_specs, check_vma=False
    )
```

```python
import functools

import jax
import jax.numpy as jnp
from jax import lax
from jax.experimental import pallas as pl
from jax.experimental.pallas import tpu as pltpu
from jax.sharding import PartitionSpec as P

GROUP = 16
TOKENS_AT_ONCE = 512
VMEM_LIMIT = 48 * 1024 * 1024


FOUR_PLACES = (
    ((2, 3), (1, 2), (0, 0), (3, 1)),
    ((1, 0), (3, 1), (2, 2), (0, 3)),
)


def plan(owners):
    if owners == 4:
        return FOUR_PLACES
    return (tuple((turn, turn) for turn in reversed(range(owners))),) * 2


def layer_norm(values, norm_gain, norm_bias):
    average = jnp.mean(values, axis=-1, keepdims=True)
    centred = values - average
    variance = jnp.mean(centred * centred, axis=-1, keepdims=True)
    return centred * lax.rsqrt(variance + 1e-05) * norm_gain + norm_bias


def normed_of(blocks, gain, bias):
    values = jnp.concatenate(blocks, axis=0).astype(jnp.float32)
    return layer_norm(values, gain[...], bias[...]).astype(jnp.bfloat16)


def gated(normed, gate_w, w):
    gate = jnp.dot(normed, gate_w[...], preferred_element_type=jnp.float32)
    value = jnp.dot(normed, w[...], preferred_element_type=jnp.float32)
    return (jax.nn.sigmoid(gate) * value).astype(jnp.bfloat16).astype(jnp.float32)


def fetch(*refs):
    count = len(refs) // 2
    sources, targets, sems = refs[:count], refs[count : 2 * count], refs[2 * count]
    copies = [
        pltpu.make_async_copy(source, target, sems.at[number])
        for number, (source, target) in enumerate(zip(sources, targets))
    ]
    for copy in copies:
        copy.start()
    for copy in copies:
        copy.wait()


def join(own, other, joined):
    col = lax.axis_index("col")
    joined[col] = own[...]
    joined[1 - col] = other[...]


def own_rows(joined, in_gain, in_bias, left_gate_w, left_w, out_gate_w, left, gating):
    col_parts, rows, cols, channels = joined.shape
    blocks = [joined[part, a] for a in range(rows) for part in range(col_parts)]
    left[...] = gated(normed_of(blocks, in_gain, in_bias), left_gate_w, left_w)
    mine = joined[lax.axis_index("col")].reshape(rows * cols, channels)
    gate = jnp.dot(
        normed_of([mine], in_gain, in_bias), out_gate_w[...], preferred_element_type=jnp.float32
    )
    gating[...] = jax.nn.sigmoid(gate)


def triangle(owners, *refs):
    blocks = refs[:owners]
    left, gating, in_gain, in_bias, right_gate_w, right_w = refs[owners : owners + 6]
    mid_gain, mid_bias, out_w, out, raw_held, right_held = refs[owners + 6 :]
    rows, cols, channels = out.shape
    col_parts = raw_held.shape[1]
    depth = cols * col_parts
    row, col = lax.axis_index("row"), lax.axis_index("col")
    at_home = row // owners == col
    for block, (first, second) in zip(blocks, reversed(list(zip(*plan(owners))))):
        turn = jnp.where(
            at_home,
            jnp.where(col == 0, first[1], second[1]),
            jnp.where(col == 0, first[0], second[0]),
        )
        raw_held[lax.bitwise_xor(lax.rem(row, owners), turn)] = block[...]

    rows_at_once = max(1, min(GROUP, TOKENS_AT_ONCE // depth))

    def one_group(group):
        for first in range(0, GROUP, rows_at_once):
            blocks = [
                raw_held[group * (GROUP // rows) + j // rows, part, j % rows]
                for j in range(first, first + rows_at_once)
                for part in range(col_parts)
            ]
            right_held[first * depth : (first + rows_at_once) * depth] = gated(
                normed_of(blocks, in_gain, in_bias), right_gate_w, right_w
            )

        def add(k, sums):
            right = right_held[pl.ds(k, GROUP, stride=depth)]
            return [sums[a] + left[pl.ds(a * depth + k, 1)] * right for a in range(rows)]

        sums = [jnp.zeros((GROUP, right_held.shape[1]), jnp.float32)] * rows
        if depth <= 32:
            for k in range(depth):
                sums = add(k, sums)
        else:
            sums = lax.fori_loop(0, depth, add, sums, unroll=8)
        middle = layer_norm(jnp.concatenate(sums, axis=0), mid_gain[...], mid_bias[...])
        update = jnp.dot(
            middle.astype(jnp.bfloat16), out_w[...], preferred_element_type=jnp.float32
        )
        for a in range(rows):
            gate = gating[pl.ds(pl.multiple_of(a * cols + group * GROUP, 8), GROUP)]
            result = gate * update[a * GROUP : (a + 1) * GROUP]
            out[a, pl.ds(pl.multiple_of(group * GROUP, GROUP), GROUP)] = result.astype(out.dtype)

    groups = cols // GROUP
    if groups == 1:
        one_group(0)
    else:
        pl.loop(0, groups)(one_group)


def on_device(pair_repr, *params):
    rows, cols, channels = pair_repr.shape
    hidden = params[3].shape[1]
    row_parts, col_parts = lax.axis_size("row"), lax.axis_size("col")
    depth = cols * col_parts
    owners = cols // rows
    f32, bf16 = jnp.float32, jnp.bfloat16
    shape = jax.ShapeDtypeStruct
    vmem = pl.BlockSpec(memory_space=pltpu.VMEM)

    def call(body, name, outs, ins, scratch=(), in_spec=vmem):
        return pl.pallas_call(
            body,
            name=name,
            out_shape=outs,
            in_specs=[in_spec] * len(ins),
            out_specs=[vmem] * len(outs),
            scratch_shapes=list(scratch),
            compiler_params=pltpu.CompilerParams(vmem_limit_bytes=VMEM_LIMIT),
        )(*ins)

    other = lax.ppermute(pair_repr, "col", [(0, 1), (1, 0)])
    sources = [pair_repr] + [p.reshape(1, -1) if p.ndim == 1 else p for p in params]
    own, *params = call(
        fetch,
        "fetch",
        [shape(source.shape, source.dtype) for source in sources],
        [pltpu.with_memory_space_constraint(source, pltpu.HBM) for source in sources],
        [pltpu.SemaphoreType.DMA((len(sources),))],
        pl.BlockSpec(memory_space=pltpu.HBM),
    )
    (
        in_gain,
        in_bias,
        left_gate_w,
        left_w,
        right_gate_w,
        right_w,
        out_gate_w,
        mid_gain,
        mid_bias,
        out_w,
    ) = params
    (joined,) = call(join, "join", [shape((col_parts,) + pair_repr.shape, bf16)], [own, other])

    blocks = []
    for step in reversed(range(owners)):
        pairs = []
        for r in range(row_parts):
            half = r // owners
            far_turn, near_turn = plan(owners)[half][step]
            far = (r ^ owners ^ far_turn) * col_parts + half
            near = (r ^ near_turn) * col_parts + half
            pairs += [(r * col_parts + half, far), (r * col_parts + 1 - half, near)]
        blocks.append(lax.ppermute(joined, ("row", "col"), pairs))

    left, gating = call(
        own_rows,
        "own_rows",
        [shape((rows * depth, hidden), f32), shape((rows * cols, channels), f32)],
        [joined, in_gain, in_bias, left_gate_w, left_w, out_gate_w],
    )
    (update,) = call(
        functools.partial(triangle, owners),
        "triangle",
        [shape(pair_repr.shape, bf16)],
        blocks
        + [left, gating, in_gain, in_bias, right_gate_w, right_w, mid_gain, mid_bias, out_w],
        [
            pltpu.VMEM((owners, col_parts) + pair_repr.shape, bf16),
            pltpu.VMEM((GROUP * depth, hidden), f32),
        ],
    )
    return update


def solution(mesh):
    in_specs = (P(("groups", "row"), "col", None), P(), P(), P(), P(), P(), P(), P(), P(), P(), P())
    out_specs = P(("groups", "row"), "col", None)
    return jax.shard_map(
        on_device, mesh=mesh, in_specs=in_specs, out_specs=out_specs, check_vma=False
    )
```

```python
import functools

import jax
import jax.numpy as jnp
import numpy as np
from jax import lax
from jax.experimental import pallas as pl
from jax.experimental.pallas import tpu as pltpu
from jax.sharding import PartitionSpec as P

GROUP = 16
TOKENS_AT_ONCE = 512
VMEM_LIMIT = 48 * 1024 * 1024


FOUR_PLACES = (
    ((4, 1, 0, 5, 3, 6, 2, 7), (6, 3, 5, 7, 4, 1, 0, 2)),
    ((5, 3, 2, 7, 1, 4, 6, 0), (5, 2, 1, 3, 6, 0, 7, 4)),
    ((7, 2, 6, 1, 5, 0, 4, 3), (4, 1, 2, 0, 7, 3, 6, 5)),
    ((6, 0, 3, 4, 7, 2, 5, 1), (0, 7, 4, 6, 5, 2, 3, 1)),
)


def sent_to(owners, step, row, col):
    half, place = row // owners, row % owners
    if owners == 4:
        return FOUR_PLACES[step][half][2 * place + col]
    return row ^ step if col != half else row ^ owners ^ step


def place_of_block(owners, step, row, col):
    if owners != 4:
        return lax.bitwise_xor(lax.rem(row, owners), step)
    packed = 0
    for half in range(2):
        for place in range(4):
            for sender in range(2):
                target = sent_to(4, step, half * 4 + place, sender)
                packed |= place << 2 * (2 * target + half)
    packed = np.array(packed, np.uint32).astype(np.int32)[()]
    return lax.shift_right_logical(packed, 2 * (2 * row + col)) & 3


def layer_norm(values, norm_gain, norm_bias):
    average = jnp.mean(values, axis=-1, keepdims=True)
    centred = values - average
    variance = jnp.mean(centred * centred, axis=-1, keepdims=True)
    return centred * lax.rsqrt(variance + 1e-05) * norm_gain + norm_bias


def normed_of(blocks, gain, bias):
    values = jnp.concatenate(blocks, axis=0).astype(jnp.float32)
    return layer_norm(values, gain[...], bias[...]).astype(jnp.bfloat16)


def gated(normed, gate_w, w):
    gate = jnp.dot(normed, gate_w[...], preferred_element_type=jnp.float32)
    value = jnp.dot(normed, w[...], preferred_element_type=jnp.float32)
    return (jax.nn.sigmoid(gate) * value).astype(jnp.bfloat16).astype(jnp.float32)


def fetch(*refs):
    count = len(refs) // 2
    sources, targets, sems = refs[:count], refs[count : 2 * count], refs[2 * count]
    copies = [
        pltpu.make_async_copy(source, target, sems.at[number])
        for number, (source, target) in enumerate(zip(sources, targets))
    ]
    for copy in copies:
        copy.start()
    for copy in copies:
        copy.wait()


def join(own, other, joined):
    col = lax.axis_index("col")
    joined[col] = own[...]
    joined[1 - col] = other[...]


def own_rows(joined, in_gain, in_bias, left_gate_w, left_w, out_gate_w, left, gating):
    col_parts, rows, cols, channels = joined.shape
    blocks = [joined[part, a] for a in range(rows) for part in range(col_parts)]
    left[...] = gated(normed_of(blocks, in_gain, in_bias), left_gate_w, left_w)
    mine = joined[lax.axis_index("col")].reshape(rows * cols, channels)
    gate = jnp.dot(
        normed_of([mine], in_gain, in_bias), out_gate_w[...], preferred_element_type=jnp.float32
    )
    gating[...] = jax.nn.sigmoid(gate)


def triangle(owners, *refs):
    blocks = refs[:owners]
    left, gating, in_gain, in_bias, right_gate_w, right_w = refs[owners : owners + 6]
    mid_gain, mid_bias, out_w, out, raw_held, right_held = refs[owners + 6 :]
    rows, cols, channels = out.shape
    col_parts = raw_held.shape[1]
    depth = cols * col_parts
    row, col = lax.axis_index("row"), lax.axis_index("col")
    for step in range(owners):
        raw_held[place_of_block(owners, step, row, col)] = blocks[owners - 1 - step][...]

    rows_at_once = max(1, min(GROUP, TOKENS_AT_ONCE // depth))

    def one_group(group):
        for first in range(0, GROUP, rows_at_once):
            blocks = [
                raw_held[group * (GROUP // rows) + j // rows, part, j % rows]
                for j in range(first, first + rows_at_once)
                for part in range(col_parts)
            ]
            right_held[first * depth : (first + rows_at_once) * depth] = gated(
                normed_of(blocks, in_gain, in_bias), right_gate_w, right_w
            )

        def add(k, sums):
            right = right_held[pl.ds(k, GROUP, stride=depth)]
            return [sums[a] + left[pl.ds(a * depth + k, 1)] * right for a in range(rows)]

        sums = [jnp.zeros((GROUP, right_held.shape[1]), jnp.float32)] * rows
        if depth <= 32:
            for k in range(depth):
                sums = add(k, sums)
        else:
            sums = lax.fori_loop(0, depth, add, sums, unroll=8)
        middle = layer_norm(jnp.concatenate(sums, axis=0), mid_gain[...], mid_bias[...])
        update = jnp.dot(
            middle.astype(jnp.bfloat16), out_w[...], preferred_element_type=jnp.float32
        )
        for a in range(rows):
            gate = gating[pl.ds(pl.multiple_of(a * cols + group * GROUP, 8), GROUP)]
            result = gate * update[a * GROUP : (a + 1) * GROUP]
            out[a, pl.ds(pl.multiple_of(group * GROUP, GROUP), GROUP)] = result.astype(out.dtype)

    groups = cols // GROUP
    if groups == 1:
        one_group(0)
    else:
        pl.loop(0, groups)(one_group)


def on_device(pair_repr, *params):
    rows, cols, channels = pair_repr.shape
    hidden = params[3].shape[1]
    row_parts, col_parts = lax.axis_size("row"), lax.axis_size("col")
    depth = cols * col_parts
    owners = cols // rows
    f32, bf16 = jnp.float32, jnp.bfloat16
    shape = jax.ShapeDtypeStruct
    vmem = pl.BlockSpec(memory_space=pltpu.VMEM)

    def call(body, name, outs, ins, scratch=(), in_spec=vmem):
        return pl.pallas_call(
            body,
            name=name,
            out_shape=outs,
            in_specs=[in_spec] * len(ins),
            out_specs=[vmem] * len(outs),
            scratch_shapes=list(scratch),
            compiler_params=pltpu.CompilerParams(vmem_limit_bytes=VMEM_LIMIT),
        )(*ins)

    other = lax.ppermute(pair_repr, "col", [(0, 1), (1, 0)])
    sources = [pair_repr] + [p.reshape(1, -1) if p.ndim == 1 else p for p in params]
    own, *params = call(
        fetch,
        "fetch",
        [shape(source.shape, source.dtype) for source in sources],
        [pltpu.with_memory_space_constraint(source, pltpu.HBM) for source in sources],
        [pltpu.SemaphoreType.DMA((len(sources),))],
        pl.BlockSpec(memory_space=pltpu.HBM),
    )
    (
        in_gain,
        in_bias,
        left_gate_w,
        left_w,
        right_gate_w,
        right_w,
        out_gate_w,
        mid_gain,
        mid_bias,
        out_w,
    ) = params
    (joined,) = call(join, "join", [shape((col_parts,) + pair_repr.shape, bf16)], [own, other])

    blocks = []
    for step in reversed(range(owners)):
        pairs = [
            (r * col_parts + c, sent_to(owners, step, r, c) * col_parts + r // owners)
            for r in range(row_parts)
            for c in range(col_parts)
        ]
        blocks.append(lax.ppermute(joined, ("row", "col"), pairs))

    left, gating = call(
        own_rows,
        "own_rows",
        [shape((rows * depth, hidden), f32), shape((rows * cols, channels), f32)],
        [joined, in_gain, in_bias, left_gate_w, left_w, out_gate_w],
    )
    (update,) = call(
        functools.partial(triangle, owners),
        "triangle",
        [shape(pair_repr.shape, bf16)],
        blocks
        + [left, gating, in_gain, in_bias, right_gate_w, right_w, mid_gain, mid_bias, out_w],
        [
            pltpu.VMEM((owners, col_parts) + pair_repr.shape, bf16),
            pltpu.VMEM((GROUP * depth, hidden), f32),
        ],
    )
    return update


def solution(mesh):
    in_specs = (P(("groups", "row"), "col", None), P(), P(), P(), P(), P(), P(), P(), P(), P(), P())
    out_specs = P(("groups", "row"), "col", None)
    return jax.shard_map(
        on_device, mesh=mesh, in_specs=in_specs, out_specs=out_specs, check_vma=False
    )
```

```python
import functools

import jax
import jax.numpy as jnp
import numpy as np
from jax import lax
from jax.experimental import pallas as pl
from jax.experimental.pallas import tpu as pltpu
from jax.sharding import PartitionSpec as P

GROUP = 16
TOKENS_AT_ONCE = 512
VMEM_LIMIT = 48 * 1024 * 1024


FOUR_PLACES = (
    ((4, 1, 0, 5, 3, 6, 2, 7), (6, 3, 5, 7, 4, 1, 0, 2)),
    ((5, 3, 2, 7, 1, 4, 6, 0), (5, 2, 1, 3, 6, 0, 7, 4)),
    ((7, 2, 6, 1, 5, 0, 4, 3), (4, 1, 2, 0, 7, 3, 6, 5)),
    ((6, 0, 3, 4, 7, 2, 5, 1), (0, 7, 4, 6, 5, 2, 3, 1)),
)


def sent_to(owners, step, row, col):
    half, place = row // owners, row % owners
    if owners == 4:
        return FOUR_PLACES[step][half][2 * place + col]
    return row ^ step if col != half else row ^ owners ^ step


def place_of_block(owners, step, row, col):
    if owners != 4:
        return lax.bitwise_xor(lax.rem(row, owners), step)
    packed = 0
    for half in range(2):
        for place in range(4):
            for sender in range(2):
                target = sent_to(4, step, half * 4 + place, sender)
                packed |= place << 2 * (2 * target + half)
    packed = np.array(packed, np.uint32).astype(np.int32)[()]
    return lax.shift_right_logical(packed, 2 * (2 * row + col)) & 3


def layer_norm(values, norm_gain, norm_bias):
    average = jnp.mean(values, axis=-1, keepdims=True)
    centred = values - average
    variance = jnp.mean(centred * centred, axis=-1, keepdims=True)
    return centred * lax.rsqrt(variance + 1e-05) * norm_gain + norm_bias


def sigmoid(values):
    return 0.5 * jnp.tanh(0.5 * values) + 0.5


def normed_of(blocks, gain, bias):
    values = jnp.concatenate(blocks, axis=0).astype(jnp.float32)
    return layer_norm(values, gain[...], bias[...]).astype(jnp.bfloat16)


def gated(normed, gate_w, w):
    gate = jnp.dot(normed, gate_w[...], preferred_element_type=jnp.float32)
    value = jnp.dot(normed, w[...], preferred_element_type=jnp.float32)
    return sigmoid(gate) * value


def fetch(*refs):
    count = len(refs) // 2
    sources, targets, sems = refs[:count], refs[count : 2 * count], refs[2 * count]
    copies = [
        pltpu.make_async_copy(source, target, sems.at[number])
        for number, (source, target) in enumerate(zip(sources, targets))
    ]
    for copy in copies:
        copy.start()
    for copy in copies:
        copy.wait()


def join(own, other, joined):
    col = lax.axis_index("col")
    joined[col] = own[...]
    joined[1 - col] = other[...]


def own_rows(joined, in_gain, in_bias, left_gate_w, left_w, out_gate_w, left, gating):
    col_parts, rows, cols, channels = joined.shape
    blocks = [joined[part, a] for a in range(rows) for part in range(col_parts)]
    left[...] = gated(normed_of(blocks, in_gain, in_bias), left_gate_w, left_w)
    mine = joined[lax.axis_index("col")].reshape(rows * cols, channels)
    gate = jnp.dot(
        normed_of([mine], in_gain, in_bias), out_gate_w[...], preferred_element_type=jnp.float32
    )
    gating[...] = sigmoid(gate)


def triangle(owners, *refs):
    blocks = refs[:owners]
    left, gating, in_gain, in_bias, right_gate_w, right_w = refs[owners : owners + 6]
    mid_gain, mid_bias, out_w, out, right_held = refs[owners + 6 :]
    rows, cols, channels = out.shape
    col_parts = blocks[0].shape[0]
    depth = cols * col_parts
    tokens = rows * depth
    row, col = lax.axis_index("row"), lax.axis_index("col")

    at_once = max(1, TOKENS_AT_ONCE // tokens)
    for begin in range(0, owners, at_once):
        some = range(begin, min(begin + at_once, owners))
        raw = [
            blocks[owners - 1 - step][part, a]
            for step in some
            for a in range(rows)
            for part in range(col_parts)
        ]
        right = gated(normed_of(raw, in_gain, in_bias), right_gate_w, right_w)
        for number, step in enumerate(some):
            start = pl.multiple_of(place_of_block(owners, step, row, col) * tokens, tokens)
            right_held[pl.ds(start, tokens)] = right[number * tokens : (number + 1) * tokens]

    def one_group(group):
        def add(k, sums):
            right = right_held[pl.ds(group * (GROUP * depth) + k, GROUP, stride=depth)]
            return [sums[a] + left[pl.ds(a * depth + k, 1)] * right for a in range(rows)]

        sums = [jnp.zeros((GROUP, right_held.shape[1]), jnp.float32)] * rows
        if depth <= 32:
            for k in range(depth):
                sums = add(k, sums)
        else:
            sums = lax.fori_loop(0, depth, add, sums, unroll=8)
        middle = layer_norm(jnp.concatenate(sums, axis=0), mid_gain[...], mid_bias[...])
        update = jnp.dot(
            middle.astype(jnp.bfloat16), out_w[...], preferred_element_type=jnp.float32
        )
        for a in range(rows):
            gate = gating[pl.ds(pl.multiple_of(a * cols + group * GROUP, 8), GROUP)]
            result = gate * update[a * GROUP : (a + 1) * GROUP]
            out[a, pl.ds(pl.multiple_of(group * GROUP, GROUP), GROUP)] = result.astype(out.dtype)

    groups = cols // GROUP
    if groups == 1:
        one_group(0)
    else:
        pl.loop(0, groups)(one_group)


def on_device(pair_repr, *params):
    rows, cols, channels = pair_repr.shape
    hidden = params[3].shape[1]
    row_parts, col_parts = lax.axis_size("row"), lax.axis_size("col")
    depth = cols * col_parts
    owners = cols // rows
    f32, bf16 = jnp.float32, jnp.bfloat16
    shape = jax.ShapeDtypeStruct
    vmem = pl.BlockSpec(memory_space=pltpu.VMEM)

    def call(body, name, outs, ins, scratch=(), in_spec=vmem):
        return pl.pallas_call(
            body,
            name=name,
            out_shape=outs,
            in_specs=[in_spec] * len(ins),
            out_specs=[vmem] * len(outs),
            scratch_shapes=list(scratch),
            compiler_params=pltpu.CompilerParams(vmem_limit_bytes=VMEM_LIMIT),
        )(*ins)

    other = lax.ppermute(pair_repr, "col", [(0, 1), (1, 0)])
    sources = [pair_repr] + [p.reshape(1, -1) if p.ndim == 1 else p for p in params]
    own, *params = call(
        fetch,
        "fetch",
        [shape(source.shape, source.dtype) for source in sources],
        [pltpu.with_memory_space_constraint(source, pltpu.HBM) for source in sources],
        [pltpu.SemaphoreType.DMA((len(sources),))],
        pl.BlockSpec(memory_space=pltpu.HBM),
    )
    (
        in_gain,
        in_bias,
        left_gate_w,
        left_w,
        right_gate_w,
        right_w,
        out_gate_w,
        mid_gain,
        mid_bias,
        out_w,
    ) = params
    (joined,) = call(join, "join", [shape((col_parts,) + pair_repr.shape, bf16)], [own, other])

    blocks = []
    for step in reversed(range(owners)):
        pairs = [
            (r * col_parts + c, sent_to(owners, step, r, c) * col_parts + r // owners)
            for r in range(row_parts)
            for c in range(col_parts)
        ]
        blocks.append(lax.ppermute(joined, ("row", "col"), pairs))

    left, gating = call(
        own_rows,
        "own_rows",
        [shape((rows * depth, hidden), f32), shape((rows * cols, channels), f32)],
        [joined, in_gain, in_bias, left_gate_w, left_w, out_gate_w],
    )
    (update,) = call(
        functools.partial(triangle, owners),
        "triangle",
        [shape(pair_repr.shape, bf16)],
        blocks
        + [left, gating, in_gain, in_bias, right_gate_w, right_w, mid_gain, mid_bias, out_w],
        [pltpu.VMEM((cols * depth, hidden), f32)],
    )
    return update


def solution(mesh):
    in_specs = (P(("groups", "row"), "col", None), P(), P(), P(), P(), P(), P(), P(), P(), P(), P())
    out_specs = P(("groups", "row"), "col", None)
    return jax.shard_map(
        on_device, mesh=mesh, in_specs=in_specs, out_specs=out_specs, check_vma=False
    )
```

```python
import functools

import jax
import jax.numpy as jnp
import numpy as np
from jax import lax
from jax.experimental import pallas as pl
from jax.experimental.pallas import tpu as pltpu
from jax.sharding import PartitionSpec as P

GROUP = 16
TOKENS_AT_ONCE = 512
VMEM_LIMIT = 48 * 1024 * 1024


FOUR_PLACES = (
    ((4, 1, 0, 5, 3, 6, 2, 7), (6, 3, 5, 7, 4, 1, 0, 2)),
    ((5, 3, 2, 7, 1, 4, 6, 0), (5, 2, 1, 3, 6, 0, 7, 4)),
    ((7, 2, 6, 1, 5, 0, 4, 3), (4, 1, 2, 0, 7, 3, 6, 5)),
    ((6, 0, 3, 4, 7, 2, 5, 1), (0, 7, 4, 6, 5, 2, 3, 1)),
)


def sent_to(owners, step, row, col):
    half, place = row // owners, row % owners
    if owners == 4:
        return FOUR_PLACES[step][half][2 * place + col]
    return row ^ step if col != half else row ^ owners ^ step


def place_of_block(owners, step, row, col):
    if owners != 4:
        return lax.bitwise_xor(lax.rem(row, owners), step)
    packed = 0
    for half in range(2):
        for place in range(4):
            for sender in range(2):
                target = sent_to(4, step, half * 4 + place, sender)
                packed |= place << 2 * (2 * target + half)
    packed = np.array(packed, np.uint32).astype(np.int32)[()]
    return lax.shift_right_logical(packed, 2 * (2 * row + col)) & 3


def layer_norm(values, norm_gain, norm_bias):
    average = jnp.mean(values, axis=-1, keepdims=True)
    centred = values - average
    variance = jnp.mean(centred * centred, axis=-1, keepdims=True)
    return centred * lax.rsqrt(variance + 1e-05) * norm_gain + norm_bias


def normed_of(blocks, gain, bias):
    values = jnp.concatenate(blocks, axis=0).astype(jnp.float32)
    return layer_norm(values, gain[...], bias[...]).astype(jnp.bfloat16)


def gated(normed, gate_w, w):
    gate = jnp.dot(normed, gate_w[...], preferred_element_type=jnp.float32)
    value = jnp.dot(normed, w[...], preferred_element_type=jnp.float32)
    return (jax.nn.sigmoid(gate) * value).astype(jnp.bfloat16).astype(jnp.float32)


def fold(pieces):
    row = lax.broadcasted_iota(jnp.int32, pieces[0].shape, 0)
    for shift in (4, 2, 1):
        keep = (row & shift) == 0
        half = len(pieces) // 2
        pieces = [
            jnp.where(keep, low + pltpu.roll(low, 8 - shift, 0), high + pltpu.roll(high, shift, 0))
            for low, high in zip(pieces[:half], pieces[half:])
        ]
    return pieces[0]


def fetch(*refs):
    count = len(refs) // 2
    sources, targets, sems = refs[:count], refs[count : 2 * count], refs[2 * count]
    copies = [
        pltpu.make_async_copy(source, target, sems.at[number])
        for number, (source, target) in enumerate(zip(sources, targets))
    ]
    for copy in copies:
        copy.start()
    for copy in copies:
        copy.wait()


def join(own, other, joined):
    col = lax.axis_index("col")
    joined[col] = own[...]
    joined[1 - col] = other[...]


def own_rows(joined, in_gain, in_bias, left_gate_w, left_w, out_gate_w, left, gating):
    col_parts, rows, cols, channels = joined.shape
    blocks = [joined[part, a] for a in range(rows) for part in range(col_parts)]
    left[...] = gated(normed_of(blocks, in_gain, in_bias), left_gate_w, left_w)
    mine = joined[lax.axis_index("col")].reshape(rows * cols, channels)
    gate = jnp.dot(
        normed_of([mine], in_gain, in_bias), out_gate_w[...], preferred_element_type=jnp.float32
    )
    gating[...] = jax.nn.sigmoid(gate)


def triangle(owners, *refs):
    blocks = refs[:owners]
    left, gating, in_gain, in_bias, right_gate_w, right_w = refs[owners : owners + 6]
    mid_gain, mid_bias, out_w, out, raw_held, right_held = refs[owners + 6 :]
    rows, cols, channels = out.shape
    col_parts = raw_held.shape[1]
    depth = cols * col_parts
    row, col = lax.axis_index("row"), lax.axis_index("col")
    for step in range(owners):
        raw_held[place_of_block(owners, step, row, col)] = blocks[owners - 1 - step][...]

    rows_at_once = max(1, min(GROUP, TOKENS_AT_ONCE // depth))

    def one_group(group):
        for first in range(0, GROUP, rows_at_once):
            blocks = [
                raw_held[group * (GROUP // rows) + j // rows, part, j % rows]
                for j in range(first, first + rows_at_once)
                for part in range(col_parts)
            ]
            right_held[first * depth : (first + rows_at_once) * depth] = gated(
                normed_of(blocks, in_gain, in_bias), right_gate_w, right_w
            )

        def add(part, first, sums):
            at = pl.multiple_of(part * 8, 8)
            lefts = [left[pl.ds(a * depth + at, 8)] for a in range(rows)]
            rights = [right_held[pl.ds((first + j) * depth + at, 8)] for j in range(8)]
            return [sums[a * 8 + j] + lefts[a] * rights[j] for a in range(rows) for j in range(8)]

        folded = []
        for first in range(0, GROUP, 8):
            sums = [jnp.zeros((8, right_held.shape[1]), jnp.float32)] * (8 * rows)
            if depth <= 32:
                for part in range(depth // 8):
                    sums = add(part, first, sums)
            else:
                sums = lax.fori_loop(
                    0, depth // 8, lambda part, sums, first=first: add(part, first, sums), sums
                )
            folded.append([fold(sums[a * 8 : a * 8 + 8]) for a in range(rows)])
        sums = [columns[a] for a in range(rows) for columns in folded]
        middle = layer_norm(jnp.concatenate(sums, axis=0), mid_gain[...], mid_bias[...])
        update = jnp.dot(
            middle.astype(jnp.bfloat16), out_w[...], preferred_element_type=jnp.float32
        )
        for a in range(rows):
            gate = gating[pl.ds(pl.multiple_of(a * cols + group * GROUP, 8), GROUP)]
            result = gate * update[a * GROUP : (a + 1) * GROUP]
            out[a, pl.ds(pl.multiple_of(group * GROUP, GROUP), GROUP)] = result.astype(out.dtype)

    groups = cols // GROUP
    if groups == 1:
        one_group(0)
    else:
        pl.loop(0, groups)(one_group)


def on_device(pair_repr, *params):
    rows, cols, channels = pair_repr.shape
    hidden = params[3].shape[1]
    row_parts, col_parts = lax.axis_size("row"), lax.axis_size("col")
    depth = cols * col_parts
    owners = cols // rows
    f32, bf16 = jnp.float32, jnp.bfloat16
    shape = jax.ShapeDtypeStruct
    vmem = pl.BlockSpec(memory_space=pltpu.VMEM)

    def call(body, name, outs, ins, scratch=(), in_spec=vmem):
        return pl.pallas_call(
            body,
            name=name,
            out_shape=outs,
            in_specs=[in_spec] * len(ins),
            out_specs=[vmem] * len(outs),
            scratch_shapes=list(scratch),
            compiler_params=pltpu.CompilerParams(vmem_limit_bytes=VMEM_LIMIT),
        )(*ins)

    other = lax.ppermute(pair_repr, "col", [(0, 1), (1, 0)])
    sources = [pair_repr] + [p.reshape(1, -1) if p.ndim == 1 else p for p in params]
    own, *params = call(
        fetch,
        "fetch",
        [shape(source.shape, source.dtype) for source in sources],
        [pltpu.with_memory_space_constraint(source, pltpu.HBM) for source in sources],
        [pltpu.SemaphoreType.DMA((len(sources),))],
        pl.BlockSpec(memory_space=pltpu.HBM),
    )
    (
        in_gain,
        in_bias,
        left_gate_w,
        left_w,
        right_gate_w,
        right_w,
        out_gate_w,
        mid_gain,
        mid_bias,
        out_w,
    ) = params
    (joined,) = call(join, "join", [shape((col_parts,) + pair_repr.shape, bf16)], [own, other])

    blocks = []
    for step in reversed(range(owners)):
        pairs = [
            (r * col_parts + c, sent_to(owners, step, r, c) * col_parts + r // owners)
            for r in range(row_parts)
            for c in range(col_parts)
        ]
        blocks.append(lax.ppermute(joined, ("row", "col"), pairs))

    left, gating = call(
        own_rows,
        "own_rows",
        [shape((rows * depth, hidden), f32), shape((rows * cols, channels), f32)],
        [joined, in_gain, in_bias, left_gate_w, left_w, out_gate_w],
    )
    (update,) = call(
        functools.partial(triangle, owners),
        "triangle",
        [shape(pair_repr.shape, bf16)],
        blocks
        + [left, gating, in_gain, in_bias, right_gate_w, right_w, mid_gain, mid_bias, out_w],
        [
            pltpu.VMEM((owners, col_parts) + pair_repr.shape, bf16),
            pltpu.VMEM((GROUP * depth, hidden), f32),
        ],
    )
    return update


def solution(mesh):
    in_specs = (P(("groups", "row"), "col", None), P(), P(), P(), P(), P(), P(), P(), P(), P(), P())
    out_specs = P(("groups", "row"), "col", None)
    return jax.shard_map(
        on_device, mesh=mesh, in_specs=in_specs, out_specs=out_specs, check_vma=False
    )
```

```python
import functools

import jax
import jax.numpy as jnp
import numpy as np
from jax import lax
from jax.experimental import pallas as pl
from jax.experimental.pallas import tpu as pltpu
from jax.sharding import PartitionSpec as P

GROUP = 16
TOKENS_AT_ONCE = 512
VMEM_LIMIT = 48 * 1024 * 1024


FOUR_PLACES = (
    ((4, 1, 0, 5, 3, 6, 2, 7), (6, 3, 5, 7, 4, 1, 0, 2)),
    ((5, 3, 2, 7, 1, 4, 6, 0), (5, 2, 1, 3, 6, 0, 7, 4)),
    ((7, 2, 6, 1, 5, 0, 4, 3), (4, 1, 2, 0, 7, 3, 6, 5)),
    ((6, 0, 3, 4, 7, 2, 5, 1), (0, 7, 4, 6, 5, 2, 3, 1)),
)


def sent_to(owners, step, row, col):
    half, place = row // owners, row % owners
    if owners == 4:
        return FOUR_PLACES[step][half][2 * place + col]
    return row ^ step if col != half else row ^ owners ^ step


def place_of_block(owners, step, row, col):
    if owners != 4:
        return lax.bitwise_xor(lax.rem(row, owners), step)
    packed = 0
    for half in range(2):
        for place in range(4):
            for sender in range(2):
                target = sent_to(4, step, half * 4 + place, sender)
                packed |= place << 2 * (2 * target + half)
    packed = np.array(packed, np.uint32).astype(np.int32)[()]
    return lax.shift_right_logical(packed, 2 * (2 * row + col)) & 3


def layer_norm(values, norm_gain, norm_bias):
    average = jnp.mean(values, axis=-1, keepdims=True)
    centred = values - average
    variance = jnp.mean(centred * centred, axis=-1, keepdims=True)
    return centred * lax.rsqrt(variance + 1e-05) * norm_gain + norm_bias


def normed_of(blocks, gain, bias):
    values = jnp.concatenate(blocks, axis=0).astype(jnp.float32)
    return layer_norm(values, gain[...], bias[...]).astype(jnp.bfloat16)


def gated(normed, gate_w, w):
    gate = jnp.dot(normed, gate_w[...], preferred_element_type=jnp.float32)
    value = jnp.dot(normed, w[...], preferred_element_type=jnp.float32)
    return (jax.nn.sigmoid(gate) * value).astype(jnp.bfloat16).astype(jnp.float32)


def fold(pieces):
    row = lax.broadcasted_iota(jnp.int32, pieces[0].shape, 0)
    for shift in (4, 2, 1):
        keep = (row & shift) == 0
        half = len(pieces) // 2
        pieces = [
            jnp.where(keep, low + pltpu.roll(low, 8 - shift, 0), high + pltpu.roll(high, shift, 0))
            for low, high in zip(pieces[:half], pieces[half:])
        ]
    return pieces[0]


def fetch(*refs):
    count = len(refs) // 2
    sources, targets, sems = refs[:count], refs[count : 2 * count], refs[2 * count]
    copies = [
        pltpu.make_async_copy(source, target, sems.at[number])
        for number, (source, target) in enumerate(zip(sources, targets))
    ]
    for copy in copies:
        copy.start()
    for copy in copies:
        copy.wait()


def join(own, other, joined):
    col = lax.axis_index("col")
    joined[col] = own[...]
    joined[1 - col] = other[...]


def own_rows(joined, in_gain, in_bias, left_gate_w, left_w, out_gate_w, left, gating):
    col_parts, rows, cols, channels = joined.shape
    blocks = [joined[part, a] for a in range(rows) for part in range(col_parts)]
    left[...] = gated(normed_of(blocks, in_gain, in_bias), left_gate_w, left_w)
    mine = joined[lax.axis_index("col")].reshape(rows * cols, channels)
    gate = jnp.dot(
        normed_of([mine], in_gain, in_bias), out_gate_w[...], preferred_element_type=jnp.float32
    )
    gating[...] = jax.nn.sigmoid(gate)


def right_sides(blocks, in_gain, in_bias, right_gate_w, right_w, store):
    col_parts, rows, cols, channels = blocks[0].shape
    tokens = rows * cols * col_parts
    at_once = max(1, TOKENS_AT_ONCE // tokens)
    for begin in range(0, len(blocks), at_once):
        some = blocks[begin : begin + at_once]
        raw = [block[part, a] for block in some for a in range(rows) for part in range(col_parts)]
        right = gated(normed_of(raw, in_gain, in_bias), right_gate_w, right_w)
        for number in range(len(some)):
            store(begin + number, right[number * tokens : (number + 1) * tokens])


def early_right(*refs):
    blocks, early = refs[:-5], refs[-1]

    def store(number, values):
        early[number] = values

    right_sides(blocks, *refs[-5:-1], store)


def triangle(owners, *refs):
    early = refs[0]
    first = early.shape[0]
    blocks = refs[1 : 1 + owners - first]
    left, gating, *params = refs[1 + owners - first : 7 + owners - first]
    mid_gain, mid_bias, out_w, out, right_held = refs[7 + owners - first :]
    rows, cols, channels = out.shape
    depth = left.shape[0] // rows
    tokens = rows * depth
    row, col = lax.axis_index("row"), lax.axis_index("col")

    def hold(step, values):
        start = pl.multiple_of(place_of_block(owners, step, row, col) * tokens, tokens)
        right_held[pl.ds(start, tokens)] = values

    for step in range(first):
        hold(step, early[step])
    right_sides(blocks, *params, lambda number, values: hold(first + number, values))

    def one_group(group):
        def add(part, begin, sums):
            at = pl.multiple_of(part * 8, 8)
            lefts = [left[pl.ds(a * depth + at, 8)] for a in range(rows)]
            first_row = (group * GROUP + begin) * depth
            rights = [
                right_held[pl.ds(pl.multiple_of(first_row + j * depth + at, 8), 8)]
                for j in range(8)
            ]
            return [sums[a * 8 + j] + lefts[a] * rights[j] for a in range(rows) for j in range(8)]

        folded = []
        for begin in range(0, GROUP, 8):
            sums = [jnp.zeros((8, right_held.shape[1]), jnp.float32)] * (8 * rows)
            if depth <= 32:
                for part in range(depth // 8):
                    sums = add(part, begin, sums)
            else:
                sums = lax.fori_loop(
                    0, depth // 8, lambda part, sums, begin=begin: add(part, begin, sums), sums
                )
            folded.append([fold(sums[a * 8 : a * 8 + 8]) for a in range(rows)])
        sums = [columns[a] for a in range(rows) for columns in folded]
        middle = layer_norm(jnp.concatenate(sums, axis=0), mid_gain[...], mid_bias[...])
        update = jnp.dot(
            middle.astype(jnp.bfloat16), out_w[...], preferred_element_type=jnp.float32
        )
        for a in range(rows):
            gate = gating[pl.ds(pl.multiple_of(a * cols + group * GROUP, 8), GROUP)]
            result = gate * update[a * GROUP : (a + 1) * GROUP]
            out[a, pl.ds(pl.multiple_of(group * GROUP, GROUP), GROUP)] = result.astype(out.dtype)

    groups = cols // GROUP
    if groups == 1:
        one_group(0)
    else:
        pl.loop(0, groups)(one_group)


def on_device(pair_repr, *params):
    rows, cols, channels = pair_repr.shape
    hidden = params[3].shape[1]
    row_parts, col_parts = lax.axis_size("row"), lax.axis_size("col")
    depth = cols * col_parts
    owners = cols // rows
    f32, bf16 = jnp.float32, jnp.bfloat16
    shape = jax.ShapeDtypeStruct
    vmem = pl.BlockSpec(memory_space=pltpu.VMEM)

    def call(body, name, outs, ins, scratch=(), in_spec=vmem):
        return pl.pallas_call(
            body,
            name=name,
            out_shape=outs,
            in_specs=[in_spec] * len(ins),
            out_specs=[vmem] * len(outs),
            scratch_shapes=list(scratch),
            compiler_params=pltpu.CompilerParams(vmem_limit_bytes=VMEM_LIMIT),
        )(*ins)

    other = lax.ppermute(pair_repr, "col", [(0, 1), (1, 0)])
    sources = [pair_repr] + [p.reshape(1, -1) if p.ndim == 1 else p for p in params]
    own, *params = call(
        fetch,
        "fetch",
        [shape(source.shape, source.dtype) for source in sources],
        [pltpu.with_memory_space_constraint(source, pltpu.HBM) for source in sources],
        [pltpu.SemaphoreType.DMA((len(sources),))],
        pl.BlockSpec(memory_space=pltpu.HBM),
    )
    (
        in_gain,
        in_bias,
        left_gate_w,
        left_w,
        right_gate_w,
        right_w,
        out_gate_w,
        mid_gain,
        mid_bias,
        out_w,
    ) = params
    (joined,) = call(join, "join", [shape((col_parts,) + pair_repr.shape, bf16)], [own, other])

    blocks = []
    for step in range(owners):
        pairs = [
            (r * col_parts + c, sent_to(owners, step, r, c) * col_parts + r // owners)
            for r in range(row_parts)
            for c in range(col_parts)
        ]
        blocks.append(lax.ppermute(joined, ("row", "col"), pairs))

    left, gating = call(
        own_rows,
        "own_rows",
        [shape((rows * depth, hidden), f32), shape((rows * cols, channels), f32)],
        [joined, in_gain, in_bias, left_gate_w, left_w, out_gate_w],
    )
    projection = [in_gain, in_bias, right_gate_w, right_w]
    first = owners // 2
    (early,) = call(
        early_right,
        "early_right",
        [shape((first, rows * depth, hidden), f32)],
        blocks[:first] + projection,
    )
    (update,) = call(
        functools.partial(triangle, owners),
        "triangle",
        [shape(pair_repr.shape, bf16)],
        [early] + blocks[first:] + [left, gating] + projection + [mid_gain, mid_bias, out_w],
        [pltpu.VMEM((cols * depth, hidden), f32)],
    )
    return update


def solution(mesh):
    in_specs = (P(("groups", "row"), "col", None), P(), P(), P(), P(), P(), P(), P(), P(), P(), P())
    out_specs = P(("groups", "row"), "col", None)
    return jax.shard_map(
        on_device, mesh=mesh, in_specs=in_specs, out_specs=out_specs, check_vma=False
    )
```

```python
import functools

import jax
import jax.numpy as jnp
import numpy as np
from jax import lax
from jax.experimental import pallas as pl
from jax.experimental.pallas import tpu as pltpu
from jax.sharding import PartitionSpec as P

GROUP = 16
TOKENS_AT_ONCE = 512
VMEM_LIMIT = 48 * 1024 * 1024


FOUR_PLACES = (
    ((4, 1, 0, 5, 3, 6, 2, 7), (6, 3, 5, 7, 4, 1, 0, 2)),
    ((5, 3, 2, 7, 1, 4, 6, 0), (5, 2, 1, 3, 6, 0, 7, 4)),
    ((7, 2, 6, 1, 5, 0, 4, 3), (4, 1, 2, 0, 7, 3, 6, 5)),
    ((6, 0, 3, 4, 7, 2, 5, 1), (0, 7, 4, 6, 5, 2, 3, 1)),
)


def sent_to(owners, step, row, col):
    half, place = row // owners, row % owners
    if owners == 4:
        return FOUR_PLACES[step][half][2 * place + col]
    return row ^ step if col != half else row ^ owners ^ step


def place_of_block(owners, step, row, col):
    if owners != 4:
        return lax.bitwise_xor(lax.rem(row, owners), step)
    packed = 0
    for half in range(2):
        for place in range(4):
            for sender in range(2):
                target = sent_to(4, step, half * 4 + place, sender)
                packed |= place << 2 * (2 * target + half)
    packed = np.array(packed, np.uint32).astype(np.int32)[()]
    return lax.shift_right_logical(packed, 2 * (2 * row + col)) & 3


def layer_norm(values, norm_gain, norm_bias):
    average = jnp.mean(values, axis=-1, keepdims=True)
    centred = values - average
    variance = jnp.mean(centred * centred, axis=-1, keepdims=True)
    return centred * lax.rsqrt(variance + 1e-05) * norm_gain + norm_bias


def normed_of(blocks, gain, bias):
    raw = jnp.concatenate(blocks, axis=0)
    channels = raw.shape[1]
    ones = jnp.ones((channels, channels), jnp.bfloat16)

    def total(values):
        return jnp.dot(values, ones, preferred_element_type=jnp.float32)

    centred = raw.astype(jnp.float32) - total(raw) * (1 / channels)
    squared = centred * centred
    high = squared.astype(jnp.bfloat16)
    low = (squared - high.astype(jnp.float32)).astype(jnp.bfloat16)
    variance = (total(high) + total(low)) * (1 / channels)
    return (centred * lax.rsqrt(variance + 1e-05) * gain[...] + bias[...]).astype(jnp.bfloat16)


def gated(normed, gate_w, w):
    gate = jnp.dot(normed, gate_w[...], preferred_element_type=jnp.float32)
    value = jnp.dot(normed, w[...], preferred_element_type=jnp.float32)
    return (jax.nn.sigmoid(gate) * value).astype(jnp.bfloat16).astype(jnp.float32)


def fold(pieces):
    row = lax.broadcasted_iota(jnp.int32, pieces[0].shape, 0)
    for shift in (4, 2, 1):
        keep = (row & shift) == 0
        half = len(pieces) // 2
        pieces = [
            jnp.where(keep, low + pltpu.roll(low, 8 - shift, 0), high + pltpu.roll(high, shift, 0))
            for low, high in zip(pieces[:half], pieces[half:])
        ]
    return pieces[0]


def fetch(*refs):
    count = len(refs) // 2
    sources, targets, sems = refs[:count], refs[count : 2 * count], refs[2 * count]
    copies = [
        pltpu.make_async_copy(source, target, sems.at[number])
        for number, (source, target) in enumerate(zip(sources, targets))
    ]
    for copy in copies:
        copy.start()
    for copy in copies:
        copy.wait()


def join(own, other, joined):
    col = lax.axis_index("col")
    joined[col] = own[...]
    joined[1 - col] = other[...]


def own_rows(joined, in_gain, in_bias, left_gate_w, left_w, out_gate_w, left, gating):
    col_parts, rows, cols, channels = joined.shape
    blocks = [joined[part, a] for a in range(rows) for part in range(col_parts)]
    left[...] = gated(normed_of(blocks, in_gain, in_bias), left_gate_w, left_w)
    mine = joined[lax.axis_index("col")].reshape(rows * cols, channels)
    gate = jnp.dot(
        normed_of([mine], in_gain, in_bias), out_gate_w[...], preferred_element_type=jnp.float32
    )
    gating[...] = jax.nn.sigmoid(gate)


def right_sides(blocks, in_gain, in_bias, right_gate_w, right_w, store):
    col_parts, rows, cols, channels = blocks[0].shape
    tokens = rows * cols * col_parts
    at_once = max(1, TOKENS_AT_ONCE // tokens)
    for begin in range(0, len(blocks), at_once):
        some = blocks[begin : begin + at_once]
        raw = [block[part, a] for block in some for a in range(rows) for part in range(col_parts)]
        right = gated(normed_of(raw, in_gain, in_bias), right_gate_w, right_w)
        for number in range(len(some)):
            store(begin + number, right[number * tokens : (number + 1) * tokens])


def early_right(*refs):
    blocks, early = refs[:-5], refs[-1]

    def store(number, values):
        early[number] = values

    right_sides(blocks, *refs[-5:-1], store)


def triangle(owners, *refs):
    early = refs[0]
    first = early.shape[0]
    blocks = refs[1 : 1 + owners - first]
    left, gating, *params = refs[1 + owners - first : 7 + owners - first]
    mid_gain, mid_bias, out_w, out, right_held = refs[7 + owners - first :]
    rows, cols, channels = out.shape
    depth = left.shape[0] // rows
    tokens = rows * depth
    row, col = lax.axis_index("row"), lax.axis_index("col")

    def hold(step, values):
        start = pl.multiple_of(place_of_block(owners, step, row, col) * tokens, tokens)
        right_held[pl.ds(start, tokens)] = values

    for step in range(first):
        hold(step, early[step])
    right_sides(blocks, *params, lambda number, values: hold(first + number, values))

    def one_group(group):
        def add(part, begin, sums):
            at = pl.multiple_of(part * 8, 8)
            lefts = [left[pl.ds(a * depth + at, 8)] for a in range(rows)]
            first_row = (group * GROUP + begin) * depth
            rights = [
                right_held[pl.ds(pl.multiple_of(first_row + j * depth + at, 8), 8)]
                for j in range(8)
            ]
            return [sums[a * 8 + j] + lefts[a] * rights[j] for a in range(rows) for j in range(8)]

        folded = []
        for begin in range(0, GROUP, 8):
            sums = [jnp.zeros((8, right_held.shape[1]), jnp.float32)] * (8 * rows)
            if depth <= 32:
                for part in range(depth // 8):
                    sums = add(part, begin, sums)
            else:
                sums = lax.fori_loop(
                    0, depth // 8, lambda part, sums, begin=begin: add(part, begin, sums), sums
                )
            folded.append([fold(sums[a * 8 : a * 8 + 8]) for a in range(rows)])
        sums = [columns[a] for a in range(rows) for columns in folded]
        middle = layer_norm(jnp.concatenate(sums, axis=0), mid_gain[...], mid_bias[...])
        update = jnp.dot(
            middle.astype(jnp.bfloat16), out_w[...], preferred_element_type=jnp.float32
        )
        for a in range(rows):
            gate = gating[pl.ds(pl.multiple_of(a * cols + group * GROUP, 8), GROUP)]
            result = gate * update[a * GROUP : (a + 1) * GROUP]
            out[a, pl.ds(pl.multiple_of(group * GROUP, GROUP), GROUP)] = result.astype(out.dtype)

    groups = cols // GROUP
    if groups == 1:
        one_group(0)
    else:
        pl.loop(0, groups)(one_group)


def on_device(pair_repr, *params):
    rows, cols, channels = pair_repr.shape
    hidden = params[3].shape[1]
    row_parts, col_parts = lax.axis_size("row"), lax.axis_size("col")
    depth = cols * col_parts
    owners = cols // rows
    f32, bf16 = jnp.float32, jnp.bfloat16
    shape = jax.ShapeDtypeStruct
    vmem = pl.BlockSpec(memory_space=pltpu.VMEM)

    def call(body, name, outs, ins, scratch=(), in_spec=vmem):
        return pl.pallas_call(
            body,
            name=name,
            out_shape=outs,
            in_specs=[in_spec] * len(ins),
            out_specs=[vmem] * len(outs),
            scratch_shapes=list(scratch),
            compiler_params=pltpu.CompilerParams(vmem_limit_bytes=VMEM_LIMIT),
        )(*ins)

    other = lax.ppermute(pair_repr, "col", [(0, 1), (1, 0)])
    sources = [pair_repr] + [p.reshape(1, -1) if p.ndim == 1 else p for p in params]
    own, *params = call(
        fetch,
        "fetch",
        [shape(source.shape, source.dtype) for source in sources],
        [pltpu.with_memory_space_constraint(source, pltpu.HBM) for source in sources],
        [pltpu.SemaphoreType.DMA((len(sources),))],
        pl.BlockSpec(memory_space=pltpu.HBM),
    )
    (
        in_gain,
        in_bias,
        left_gate_w,
        left_w,
        right_gate_w,
        right_w,
        out_gate_w,
        mid_gain,
        mid_bias,
        out_w,
    ) = params
    (joined,) = call(join, "join", [shape((col_parts,) + pair_repr.shape, bf16)], [own, other])

    blocks = []
    for step in range(owners):
        pairs = [
            (r * col_parts + c, sent_to(owners, step, r, c) * col_parts + r // owners)
            for r in range(row_parts)
            for c in range(col_parts)
        ]
        blocks.append(lax.ppermute(joined, ("row", "col"), pairs))

    left, gating = call(
        own_rows,
        "own_rows",
        [shape((rows * depth, hidden), f32), shape((rows * cols, channels), f32)],
        [joined, in_gain, in_bias, left_gate_w, left_w, out_gate_w],
    )
    projection = [in_gain, in_bias, right_gate_w, right_w]
    first = owners // 2
    (early,) = call(
        early_right,
        "early_right",
        [shape((first, rows * depth, hidden), f32)],
        blocks[:first] + projection,
    )
    (update,) = call(
        functools.partial(triangle, owners),
        "triangle",
        [shape(pair_repr.shape, bf16)],
        [early] + blocks[first:] + [left, gating] + projection + [mid_gain, mid_bias, out_w],
        [pltpu.VMEM((cols * depth, hidden), f32)],
    )
    return update


def solution(mesh):
    in_specs = (P(("groups", "row"), "col", None), P(), P(), P(), P(), P(), P(), P(), P(), P(), P())
    out_specs = P(("groups", "row"), "col", None)
    return jax.shard_map(
        on_device, mesh=mesh, in_specs=in_specs, out_specs=out_specs, check_vma=False
    )
```

```python
import functools

import jax
import jax.numpy as jnp
import numpy as np
from jax import lax
from jax.experimental import pallas as pl
from jax.experimental.pallas import tpu as pltpu
from jax.sharding import PartitionSpec as P

GROUP = 16
TOKENS_AT_ONCE = 512
VMEM_LIMIT = 48 * 1024 * 1024


FOUR_PLACES = (
    ((4, 1, 0, 5, 3, 6, 2, 7), (6, 3, 5, 7, 4, 1, 0, 2)),
    ((5, 3, 2, 7, 1, 4, 6, 0), (5, 2, 1, 3, 6, 0, 7, 4)),
    ((7, 2, 6, 1, 5, 0, 4, 3), (4, 1, 2, 0, 7, 3, 6, 5)),
    ((6, 0, 3, 4, 7, 2, 5, 1), (0, 7, 4, 6, 5, 2, 3, 1)),
)


def sent_to(owners, step, row, col):
    half, place = row // owners, row % owners
    if owners == 4:
        return FOUR_PLACES[step][half][2 * place + col]
    return row ^ step if col != half else row ^ owners ^ step


def place_of_block(owners, step, row, col):
    if owners != 4:
        return lax.bitwise_xor(lax.rem(row, owners), step)
    packed = 0
    for half in range(2):
        for place in range(4):
            for sender in range(2):
                target = sent_to(4, step, half * 4 + place, sender)
                packed |= place << 2 * (2 * target + half)
    packed = np.array(packed, np.uint32).astype(np.int32)[()]
    return lax.shift_right_logical(packed, 2 * (2 * row + col)) & 3


def layer_norm(values, norm_gain, norm_bias):
    average = jnp.mean(values, axis=-1, keepdims=True)
    centred = values - average
    variance = jnp.mean(centred * centred, axis=-1, keepdims=True)
    return centred * lax.rsqrt(variance + 1e-05) * norm_gain + norm_bias


def normed_of(blocks, gain, bias):
    values = jnp.concatenate(blocks, axis=0).astype(jnp.float32)
    return layer_norm(values, gain[...], bias[...]).astype(jnp.bfloat16)


def gated(normed, gate_w, w):
    weights = jnp.concatenate([gate_w[...], w[...]], axis=1)
    both = jnp.dot(normed, weights, preferred_element_type=jnp.float32)
    hidden = both.shape[1] // 2
    product = jax.nn.sigmoid(both[:, :hidden]) * both[:, hidden:]
    return product.astype(jnp.bfloat16).astype(jnp.float32)


def fold(pieces):
    row = lax.broadcasted_iota(jnp.int32, pieces[0].shape, 0)
    for shift in (4, 2, 1):
        keep = (row & shift) == 0
        half = len(pieces) // 2
        pieces = [
            jnp.where(keep, low + pltpu.roll(low, 8 - shift, 0), high + pltpu.roll(high, shift, 0))
            for low, high in zip(pieces[:half], pieces[half:])
        ]
    return pieces[0]


def fetch(*refs):
    count = len(refs) // 2
    sources, targets, sems = refs[:count], refs[count : 2 * count], refs[2 * count]
    copies = [
        pltpu.make_async_copy(source, target, sems.at[number])
        for number, (source, target) in enumerate(zip(sources, targets))
    ]
    for copy in copies:
        copy.start()
    for copy in copies:
        copy.wait()


def join(own, other, joined):
    col = lax.axis_index("col")
    joined[col] = own[...]
    joined[1 - col] = other[...]


def own_rows(joined, in_gain, in_bias, left_gate_w, left_w, out_gate_w, left, gating):
    col_parts, rows, cols, channels = joined.shape
    blocks = [joined[part, a] for a in range(rows) for part in range(col_parts)]
    left[...] = gated(normed_of(blocks, in_gain, in_bias), left_gate_w, left_w)
    mine = joined[lax.axis_index("col")].reshape(rows * cols, channels)
    gate = jnp.dot(
        normed_of([mine], in_gain, in_bias), out_gate_w[...], preferred_element_type=jnp.float32
    )
    gating[...] = jax.nn.sigmoid(gate)


def right_sides(blocks, in_gain, in_bias, right_gate_w, right_w, store):
    col_parts, rows, cols, channels = blocks[0].shape
    tokens = rows * cols * col_parts
    at_once = max(1, TOKENS_AT_ONCE // tokens)
    for begin in range(0, len(blocks), at_once):
        some = blocks[begin : begin + at_once]
        raw = [block[part, a] for block in some for a in range(rows) for part in range(col_parts)]
        right = gated(normed_of(raw, in_gain, in_bias), right_gate_w, right_w)
        for number in range(len(some)):
            store(begin + number, right[number * tokens : (number + 1) * tokens])


def early_right(*refs):
    blocks, early = refs[:-5], refs[-1]

    def store(number, values):
        early[number] = values

    right_sides(blocks, *refs[-5:-1], store)


def triangle(owners, *refs):
    early = refs[0]
    first = early.shape[0]
    blocks = refs[1 : 1 + owners - first]
    left, gating, *params = refs[1 + owners - first : 7 + owners - first]
    mid_gain, mid_bias, out_w, out, right_held = refs[7 + owners - first :]
    rows, cols, channels = out.shape
    depth = left.shape[0] // rows
    tokens = rows * depth
    row, col = lax.axis_index("row"), lax.axis_index("col")

    def hold(step, values):
        start = pl.multiple_of(place_of_block(owners, step, row, col) * tokens, tokens)
        right_held[pl.ds(start, tokens)] = values

    for step in range(first):
        hold(step, early[step])
    right_sides(blocks, *params, lambda number, values: hold(first + number, values))

    def one_group(group):
        def add(part, begin, sums):
            at = pl.multiple_of(part * 8, 8)
            lefts = [left[pl.ds(a * depth + at, 8)] for a in range(rows)]
            first_row = (group * GROUP + begin) * depth
            rights = [
                right_held[pl.ds(pl.multiple_of(first_row + j * depth + at, 8), 8)]
                for j in range(8)
            ]
            return [sums[a * 8 + j] + lefts[a] * rights[j] for a in range(rows) for j in range(8)]

        folded = []
        for begin in range(0, GROUP, 8):
            sums = [jnp.zeros((8, right_held.shape[1]), jnp.float32)] * (8 * rows)
            if depth <= 32:
                for part in range(depth // 8):
                    sums = add(part, begin, sums)
            else:
                sums = lax.fori_loop(
                    0, depth // 8, lambda part, sums, begin=begin: add(part, begin, sums), sums
                )
            folded.append([fold(sums[a * 8 : a * 8 + 8]) for a in range(rows)])
        sums = [columns[a] for a in range(rows) for columns in folded]
        middle = layer_norm(jnp.concatenate(sums, axis=0), mid_gain[...], mid_bias[...])
        update = jnp.dot(
            middle.astype(jnp.bfloat16), out_w[...], preferred_element_type=jnp.float32
        )
        for a in range(rows):
            gate = gating[pl.ds(pl.multiple_of(a * cols + group * GROUP, 8), GROUP)]
            result = gate * update[a * GROUP : (a + 1) * GROUP]
            out[a, pl.ds(pl.multiple_of(group * GROUP, GROUP), GROUP)] = result.astype(out.dtype)

    groups = cols // GROUP
    if groups == 1:
        one_group(0)
    else:
        pl.loop(0, groups)(one_group)


def on_device(pair_repr, *params):
    rows, cols, channels = pair_repr.shape
    hidden = params[3].shape[1]
    row_parts, col_parts = lax.axis_size("row"), lax.axis_size("col")
    depth = cols * col_parts
    owners = cols // rows
    f32, bf16 = jnp.float32, jnp.bfloat16
    shape = jax.ShapeDtypeStruct
    vmem = pl.BlockSpec(memory_space=pltpu.VMEM)

    def call(body, name, outs, ins, scratch=(), in_spec=vmem):
        return pl.pallas_call(
            body,
            name=name,
            out_shape=outs,
            in_specs=[in_spec] * len(ins),
            out_specs=[vmem] * len(outs),
            scratch_shapes=list(scratch),
            compiler_params=pltpu.CompilerParams(vmem_limit_bytes=VMEM_LIMIT),
        )(*ins)

    other = lax.ppermute(pair_repr, "col", [(0, 1), (1, 0)])
    sources = [pair_repr] + [p.reshape(1, -1) if p.ndim == 1 else p for p in params]
    own, *params = call(
        fetch,
        "fetch",
        [shape(source.shape, source.dtype) for source in sources],
        [pltpu.with_memory_space_constraint(source, pltpu.HBM) for source in sources],
        [pltpu.SemaphoreType.DMA((len(sources),))],
        pl.BlockSpec(memory_space=pltpu.HBM),
    )
    (
        in_gain,
        in_bias,
        left_gate_w,
        left_w,
        right_gate_w,
        right_w,
        out_gate_w,
        mid_gain,
        mid_bias,
        out_w,
    ) = params
    (joined,) = call(join, "join", [shape((col_parts,) + pair_repr.shape, bf16)], [own, other])

    blocks = []
    for step in range(owners):
        pairs = [
            (r * col_parts + c, sent_to(owners, step, r, c) * col_parts + r // owners)
            for r in range(row_parts)
            for c in range(col_parts)
        ]
        blocks.append(lax.ppermute(joined, ("row", "col"), pairs))

    left, gating = call(
        own_rows,
        "own_rows",
        [shape((rows * depth, hidden), f32), shape((rows * cols, channels), f32)],
        [joined, in_gain, in_bias, left_gate_w, left_w, out_gate_w],
    )
    projection = [in_gain, in_bias, right_gate_w, right_w]
    first = owners // 2
    (early,) = call(
        early_right,
        "early_right",
        [shape((first, rows * depth, hidden), f32)],
        blocks[:first] + projection,
    )
    (update,) = call(
        functools.partial(triangle, owners),
        "triangle",
        [shape(pair_repr.shape, bf16)],
        [early] + blocks[first:] + [left, gating] + projection + [mid_gain, mid_bias, out_w],
        [pltpu.VMEM((cols * depth, hidden), f32)],
    )
    return update


def solution(mesh):
    in_specs = (P(("groups", "row"), "col", None), P(), P(), P(), P(), P(), P(), P(), P(), P(), P())
    out_specs = P(("groups", "row"), "col", None)
    return jax.shard_map(
        on_device, mesh=mesh, in_specs=in_specs, out_specs=out_specs, check_vma=False
    )
```
